256 devices in a mesh: dp: 64 (over z, y, x_hi), fsdp: 4 (over x_lo, core).
Axes of the slice: x: 4 (x_hi: 2, x_lo: 2; x = x_hi * 2 + x_lo), y: 4, z: 8, core: 2. Of those that a mesh axis runs over, the one named last changes fastest.
Arguments:
- images: float32 [256, 14, 14, 768], P(('dp', 'fsdp')), may hold values from -6 to 6
- dw_kernel: float32 [7, 7, 768], replicated, may hold values from -0.875 to 0.875
- norm_gain: float32 [768], replicated, may hold values from 0.5 to 1.5
- up_weight: float32 [768, 1536], P(None, 'fsdp'), may hold values from -0.21875 to 0.21875
- up_bias: float32 [1536], P('fsdp'), may hold values from -3 to 3
- down_weight: float32 [1536, 768], P('fsdp'), may hold values from -0.15625 to 0.15625
- layer_scale: float32 [768], replicated, may hold values from 0.5 to 1.5
- projection: float32 [768, 1152], replicated, may hold values from -0.21875 to 0.21875
- text_embed: float32 [256, 1152], P(('dp', 'fsdp')), may hold values from -0.18 to 0.18
- logit_scale: float32 [], replicated, may hold values from 4 to 12
- logit_bias: float32 [], replicated, may hold values from -4 to -2
Outputs:
- input_grad: float32 [256, 14, 14, 768], P(('dp', 'fsdp'))
- up_grad: float32 [64, 768, 1536], P('dp', None, 'fsdp')
- down_grad: float32 [64, 1536, 768], P('dp', 'fsdp')
- text_grad: float32 [256, 1152], P(('dp', 'fsdp'))
- loss_rows: float32 [256], P(('dp', 'fsdp'))
The draws below stay inside these ranges and needn't reach their ends.
All inputs are finite; a program needn't handle non-finite values.
Results may differ from the reference program's by a relative error of at most 0.00026.
Values sent between devices are 32-bit elements; how exact they have to be, the bound alone decides.
No kernel may reach another device: no remote copies, remote signals or barrier semaphores. Data moves between devices by JAX's collectives and lax.ppermute only.
A program may use at most 128 MiB of HBM per device.

```python
import jax
import jax.numpy as jnp
from jax import lax

D = 768
FF = 1536
E = 1152
KS = 7
SIDE = 14
IMG_DEV = 1
BATCH = 256
N_DP = 64
N_FSDP = 4


def steps_of(key, dims, split, smallest, top_value):
    def one(dim, parts):
        steps = jax.random.uniform(jax.random.fold_in(jax.random.fold_in(key, 6), dim), (parts,), jnp.float32, smallest / len(split), top_value / len(split))
        return jnp.repeat(jnp.exp(steps), dims[dim] // parts).reshape((-1,) + (1,) * (len(dims) - dim - 1))

    factor_of = one(*split[0])
    for cut in split[1:]:
        factor_of = factor_of * one(*cut)
    return factor_of


def normal_values(own_key, shape, deviation, bound, split=(), kind=jnp.bfloat16):
    drawn = jax.random.normal(own_key, shape, jnp.float32) * deviation
    if len(split) > 0:
        drawn = steps_of(own_key, shape, split, -0.22, 0.18) * drawn
    return jnp.clip(drawn, min=-bound, max=bound).astype(kind)


def setup_inputs(seed: int = 0) -> dict:
    key_list = jax.random.split(jax.random.key(seed), 12)
    return {
        "images": normal_values(key_list[0], (BATCH, SIDE, SIDE, D), 1.0, 6.0, ((0, 256),), jnp.float32),
        "dw_kernel": normal_values(key_list[1], (KS, KS, D), (KS * KS) ** -0.5, 0.875, (), jnp.float32),
        "norm_gain": jnp.clip(1.0 + 0.1 * jax.random.normal(key_list[2], (D,), jnp.float32), 0.5, 1.5),
        "up_weight": normal_values(key_list[3], (D, FF), D ** -0.5, 0.21875, ((1, 4),), jnp.float32),
        "up_bias": normal_values(key_list[4], (FF,), 0.5, 3.0, ((0, 4),), jnp.float32),
        "down_weight": normal_values(key_list[5], (FF, D), FF ** -0.5, 0.15625, ((0, 4),), jnp.float32),
        "layer_scale": jnp.clip(1.0 + 0.1 * jax.random.normal(key_list[6], (D,), jnp.float32), 0.5, 1.5),
        "projection": normal_values(key_list[7], (D, E), D ** -0.5, 0.21875, (), jnp.float32),
        "text_embed": normal_values(key_list[8], (BATCH, E), 0.03, 0.18, ((0, 256),), jnp.float32),
        "logit_scale": jnp.clip(jax.random.uniform(key_list[9], (), jnp.float32, 4.0, 12.0), 4.0, 12.0),
        "logit_bias": jnp.clip(jax.random.uniform(key_list[10], (), jnp.float32, -4.0, -2.0), -4.0, -2.0),
    }


def conv_norm(images, dw_kernel, norm_gain):
    height = images.shape[1]
    width = images.shape[2]
    reach = dw_kernel.shape[0] // 2
    padded = jnp.pad(images, ((0, 0), (reach, reach), (reach, reach), (0, 0)))
    mixed = jnp.zeros_like(images)
    for row in range(dw_kernel.shape[0]):
        for column in range(dw_kernel.shape[1]):
            mixed = mixed + padded[:, row:row + height, column:column + width, :] * dw_kernel[row, column]
    center = lax.optimization_barrier(jnp.mean(mixed, axis=-1, keepdims=True))
    spread = lax.optimization_barrier(jnp.mean(jnp.square(mixed - center), axis=-1, keepdims=True))
    return (mixed - center) * lax.rsqrt(spread + 1e-06) * norm_gain

def pointwise(flat, first, bias_first, second):
    hidden_pre = jnp.dot(flat, first, precision=lax.Precision.HIGHEST, preferred_element_type=jnp.float32) + bias_first
    activated = jax.nn.gelu(hidden_pre, approximate=False)
    return jnp.dot(activated, second, precision=lax.Precision.HIGHEST, preferred_element_type=jnp.float32)

def pool_project(section_out, projection):
    pooled = lax.optimization_barrier(jnp.mean(section_out, axis=(1, 2)))
    return jnp.dot(pooled, projection, precision=lax.Precision.HIGHEST, preferred_element_type=jnp.float32)

def unit(vectors):
    return vectors * lax.rsqrt(lax.optimization_barrier(jnp.sum(vectors * vectors, axis=-1, keepdims=True)) + 1e-06)

def reference(images, dw_kernel, norm_gain, up_weight, up_bias, down_weight, layer_scale, projection, text_embed, logit_scale, logit_bias):
    group = N_FSDP * IMG_DEV

    def tower(block_images, first, second):
        normed = conv_norm(block_images, dw_kernel, norm_gain)
        branch = pointwise(normed.reshape(-1, D), first, up_bias, second).reshape(block_images.shape)
        return pool_project(block_images + layer_scale * branch, projection)
    grouped = images.reshape(N_DP, group, SIDE, SIDE, D)
    features = lax.map(lambda block_images: tower(block_images, up_weight, down_weight), grouped).reshape(BATCH, E)

    def objective(features, text_embed):
        image_unit = unit(features)
        text_unit = unit(text_embed)
        logits = logit_scale * jnp.dot(image_unit, text_unit.T, precision=lax.Precision.HIGHEST, preferred_element_type=jnp.float32) + logit_bias
        signs = 2.0 * jnp.eye(BATCH, dtype=logits.dtype) - 1.0
        return lax.optimization_barrier(jnp.sum(jax.nn.softplus(-signs * logits), axis=1))
    loss_rows, objective_back = jax.vjp(objective, features, text_embed)
    feature_grad, text_grad = objective_back(jnp.ones_like(loss_rows))

    def group_back(pair):
        block_images, block_grad = pair
        unused, tower_back = jax.vjp(tower, block_images, up_weight, down_weight)
        return tower_back(block_grad)
    input_grad, up_grad, down_grad = lax.map(group_back, (grouped, feature_grad.reshape(N_DP, group, E)))
    return (input_grad.reshape(BATCH, SIDE, SIDE, D), up_grad, down_grad, text_grad, loss_rows)
```

```python
import functools

import jax
import jax.numpy as jnp
from jax import lax
from jax.experimental import pallas as pl
from jax.experimental.pallas import tpu as pltpu
from jax.sharding import PartitionSpec as P

LANES = 128
HIGH = lax.Precision.HIGH
HIGHEST = lax.Precision.HIGHEST
VMEM = pl.BlockSpec(memory_space=pltpu.VMEM)
SMEM = pl.BlockSpec(memory_space=pltpu.SMEM)
F32 = jnp.float32


HBM = pl.BlockSpec(memory_space=pltpu.HBM)


def call(kernel, outs, specs, scratch=(), mib=24, flops=0, moved=0):
    return pl.pallas_call(
        kernel,
        out_shape=[jax.ShapeDtypeStruct(shape, F32) for shape in outs],
        in_specs=specs,
        out_specs=[VMEM] * len(outs),
        scratch_shapes=list(scratch),
        compiler_params=pltpu.CompilerParams(vmem_limit_bytes=mib << 20),
        cost_estimate=pl.CostEstimate(flops=flops, bytes_accessed=moved, transcendentals=0),
    )


def fetch(pairs, sems):
    copies = [
        pltpu.make_async_copy(source, target, sems.at[i])
        for i, (source, target) in enumerate(pairs)
    ]
    for copy in copies:
        copy.start()
    return copies


def dot(left, right, precision, dims=((1,), (0,))):
    return lax.dot_general(
        left, right, (dims, ((), ())), precision=precision, preferred_element_type=F32
    )


def lanes_of(tile):
    return pl.ds(pl.multiple_of(tile * LANES, LANES), LANES)


def convolve(pad, w_ref, tile, side, flip):
    taps = w_ref.shape[0]
    halves = []
    for half in range(2):
        total = jnp.zeros((side, 8, LANES), F32)
        for q in range(taps):
            column = pad[tile, :, pl.ds(q + 8 * half, 8), :]
            for p in range(taps):
                row = taps - 1 - p if flip else p
                col = taps - 1 - q if flip else q
                total = total + column[p : p + side] * w_ref[row, pl.ds(col, 1), lanes_of(tile)]
        halves.append(total)
    return halves


def front_kernel(
    x_hbm, w_hbm, gain_hbm, normed_ref, unit_ref, rstd_ref, sum_ref, x_ref, w_ref, gain_ref, pad, mixed, sems
):
    tiles, side = unit_ref.shape[0], unit_ref.shape[1]
    reach = w_ref.shape[0] // 2
    channels = tiles * LANES
    copies = fetch(((x_hbm, x_ref), (w_hbm, w_ref), (gain_hbm, gain_ref.at[0])), sems)
    pad[...] = jnp.zeros_like(pad)
    for copy in copies:
        copy.wait()
    for tile in range(tiles):
        total = jnp.zeros((side, LANES), F32)
        for h in range(side):
            row = x_ref[pl.ds(h * side * tiles + tile, side, stride=tiles), :]
            pad[tile, reach + h, pl.ds(reach, side), :] = row
            total = total + row
        sum_ref[:, tile * LANES : (tile + 1) * LANES] = jnp.sum(total, axis=0, keepdims=True)

    @pl.loop(0, tiles)
    def _(tile):
        low, high = convolve(pad, w_ref, tile, side, False)
        mixed[tile, :, 0:8, :] = low
        mixed[tile, :, 8:16, :] = high

    total = mixed[0]
    for tile in range(1, tiles):
        total = total + mixed[tile]
    mean = jnp.sum(total, axis=-1, keepdims=True) * (1.0 / channels)
    square = jnp.zeros((side, 16, LANES), F32)
    for tile in range(tiles):
        off = mixed[tile] - mean
        square = square + off * off
    rstd = lax.rsqrt(jnp.sum(square, axis=-1, keepdims=True) * (1.0 / channels) + 1e-06)
    rstd_ref[...] = jnp.broadcast_to(rstd, rstd_ref.shape)
    for tile in range(tiles):
        lanes = slice(tile * LANES, (tile + 1) * LANES)
        unit = (mixed[tile] - mean) * rstd
        unit_ref[tile] = unit
        out = unit * gain_ref[:, lanes]
        for h in range(side):
            normed_ref[h * side : (h + 1) * side, lanes] = out[h, :side]


def front(images, dw_kernel, norm_gain):
    side, taps = images.shape[1], dw_kernel.shape[0]
    channels = images.shape[3]
    tiles = channels // LANES
    return call(
        front_kernel,
        [(side * side, channels), (tiles, side, 16, LANES), (side, 16, LANES), (1, channels)],
        [HBM] * 3,
        [
            pltpu.VMEM((side * side * tiles, LANES), F32),
            pltpu.VMEM(dw_kernel.shape, F32),
            pltpu.VMEM((1, channels), F32),
            pltpu.VMEM((tiles, side + taps - 1, 24, LANES), F32),
            pltpu.VMEM((tiles, side, 16, LANES), F32),
            pltpu.SemaphoreType.DMA((3,)),
        ],
        mib=16,
        flops=side * side * channels * 2 * taps * taps,
        moved=8 * images.size,
    )(images.reshape(-1, LANES), dw_kernel, norm_gain)


def mlp_kernel(
    own_ref, across_ref, up_hbm, up_sib_ref, bias_hbm, bias_sib_hbm, down_hbm, down_sib_ref, scale_hbm, sum_ref,
    slope_ref, hidden_ref, part_ref, up_ref, bias_ref, down_ref, scale_ref, sems,
):
    positions = slope_ref.shape[2]
    width = up_ref.shape[1]
    copies = fetch(
        (
            (up_hbm, up_ref),
            (bias_hbm, bias_ref.at[0]),
            (bias_sib_hbm, bias_ref.at[1]),
            (down_hbm, down_ref),
            (scale_hbm, scale_ref.at[0]),
        ),
        sems,
    )
    for copy in copies[:3]:
        copy.wait()
    for k, normed in enumerate((own_ref, across_ref)):
        for s, weight in enumerate((up_ref, up_sib_ref)):
            pre = dot(normed[...], weight[...], HIGH) + bias_ref[pl.ds(s, 1), :]
            cdf = 0.5 * (1.0 + lax.erf(pre * (0.5**0.5)))
            slope_ref[k, s] = cdf + pre * (jnp.exp(-0.5 * pre * pre) * 0.3989422804014327)
            hidden_ref[pl.ds(k, 1), s * width : (s + 1) * width] = jnp.sum(
                pre * cdf, axis=0, keepdims=True
            )
    for copy in copies[3:]:
        copy.wait()
    hidden = hidden_ref[...]
    part = dot(hidden[:, :width], down_ref[...], HIGH) + dot(hidden[:, width:], down_sib_ref[...], HIGH)
    part = part * scale_ref[...]
    own = lax.broadcasted_iota(jnp.int32, part.shape, 0) == 0
    part = part + jnp.where(own, sum_ref[...], 0.0)
    part_ref[...] = part * (1.0 / positions)


def mlp(own, across, up, up_sib, bias, bias_sib, down, down_sib, scale, image_sum):
    positions, channels = own.shape
    hidden = up.shape[1]
    return call(
        mlp_kernel,
        [(2, 2, positions, hidden), (2, 2 * hidden), (2, channels)],
        [VMEM, VMEM, HBM, VMEM, HBM, HBM, HBM, VMEM, HBM, VMEM],
        [
            pltpu.VMEM(up.shape, F32),
            pltpu.VMEM((2, hidden), F32),
            pltpu.VMEM(down.shape, F32),
            pltpu.VMEM((1, channels), F32),
            pltpu.SemaphoreType.DMA((5,)),
        ],
        mib=24,
        flops=24 * positions * channels * hidden,
        moved=4 * (2 * positions * (channels + 2 * hidden) + 4 * channels * hidden),
    )(own, across, up, up_sib, bias, bias_sib, down, down_sib, scale, image_sum)


def normal(rows):
    inverse = lax.rsqrt(jnp.sum(rows * rows, axis=-1, keepdims=True) + 1e-06)
    return rows * inverse, inverse


def pair_kernel(
    mine_ref, other_ref, proj_hbm, texts_ref, texts_sib_ref, dp_ref, scale_ref, shift_ref,
    unit_ref, spread_ref, inverse_ref, packed_ref, proj_ref, pooled, sems,
):
    copies = fetch(((proj_hbm, proj_ref),), sems)
    embed = unit_ref.shape[1]
    text, _ = normal(texts_ref[...])
    text_sib, _ = normal(texts_sib_ref[...])
    pooled[pl.ds(0, 1), :] = mine_ref[pl.ds(0, 1), :] + other_ref[pl.ds(1, 1), :]
    pooled[pl.ds(1, 1), :] = mine_ref[pl.ds(1, 1), :] + other_ref[pl.ds(0, 1), :]
    for copy in copies:
        copy.wait()
    unit, inverse = normal(dot(pooled[...], proj_ref[...], HIGH))
    unit_ref[...] = unit
    inverse_ref[...] = jnp.broadcast_to(inverse, inverse_ref.shape)
    spread_ref[...] = jnp.broadcast_to(unit[0:1], spread_ref.shape)
    step = jnp.zeros(unit.shape, F32)
    losses = jnp.zeros((2, 1), F32)
    for s, block in enumerate((text, text_sib)):
        logits = scale_ref[0] * dot(unit, block, HIGH, ((1,), (1,))) + shift_ref[0]
        if s == 0:
            columns = lax.broadcasted_iota(jnp.int32, logits.shape, 1)
            place = lax.broadcasted_iota(jnp.int32, logits.shape, 0)
            match = jnp.where((place == 0) & (columns == dp_ref[0]), 1.0, 0.0)
        else:
            match = jnp.zeros(logits.shape, F32)
        flipped = (1.0 - 2.0 * match) * logits
        tail = jnp.log1p(jnp.exp(-jnp.abs(flipped)))
        losses = losses + jnp.sum(jnp.maximum(flipped, 0.0) + tail, axis=1, keepdims=True)
        slopes = 1.0 / (1.0 + jnp.exp(-logits)) - match
        step = step + dot(slopes, block, HIGH)
    packed_ref[:, :embed] = step * scale_ref[0]
    packed_ref[:, embed:] = jnp.broadcast_to(losses, (2, LANES))


def pairs(mine, other, projection, texts, texts_sib, dp, scale, shift):
    embed = projection.shape[1]
    return call(
        pair_kernel,
        [(2, embed), texts.shape, (2, LANES), (2, embed + LANES)],
        [VMEM, VMEM, HBM, VMEM, VMEM, SMEM, SMEM, SMEM],
        [
            pltpu.VMEM(projection.shape, F32),
            pltpu.VMEM(mine.shape, F32),
            pltpu.SemaphoreType.DMA((1,)),
        ],
        mib=16,
        flops=6 * 256 * projection.size,
        moved=4 * projection.size,
    )(mine, other, projection, texts, texts_sib, dp, scale, shift)


def slope_kernel(
    packed_ref, other_ref, unit_ref, inverse_ref, proj_hbm, scale_hbm, down_hbm, down_sib_ref, up_hbm, up_sib_ref,
    slope_ref, loss_ref, const_ref, branch_ref, grad_ref, out_ref,
    proj_ref, scale_ref, down_ref, up_ref, sums, sems,
):
    copies = fetch(
        ((proj_hbm, proj_ref), (scale_hbm, scale_ref.at[0]), (down_hbm, down_ref), (up_hbm, up_ref)), sems
    )
    embed = unit_ref.shape[1]
    width = down_ref.shape[0]
    positions = slope_ref.shape[2]
    sums[pl.ds(0, 1), :] = packed_ref[pl.ds(0, 1), :] + other_ref[pl.ds(1, 1), :]
    sums[pl.ds(1, 1), :] = packed_ref[pl.ds(1, 1), :] + other_ref[pl.ds(0, 1), :]
    loss_ref[...] = sums[0:1, embed:]
    step = sums[:, :embed]
    unit = unit_ref[...]
    grad = inverse_ref[:, 0:1] * (step - unit * jnp.sum(unit * step, axis=-1, keepdims=True))
    copies[0].wait()
    const = dot(grad, proj_ref[...], HIGH, ((1,), (1,))) * (1.0 / positions)
    const_ref[...] = const[0:1]
    copies[1].wait()
    branch = const * scale_ref[...]
    branch_ref[...] = branch
    copies[2].wait()
    grad_ref[:, :width] = dot(branch, down_ref[...], HIGH, ((1,), (1,)))
    grad_ref[:, width:] = dot(branch, down_sib_ref[...], HIGH, ((1,), (1,)))
    copies[3].wait()
    out_ref[...] = dot(
        slope_ref[1, 0] * grad_ref[1:2, :width], up_ref[...], HIGH, ((1,), (1,))
    ) + dot(slope_ref[1, 1] * grad_ref[1:2, width:], up_sib_ref[...], HIGH, ((1,), (1,)))


def slopes_of(packed, other, unit, inverse, projection, scale, down, down_sib, up, up_sib, slope):
    channels, embed = projection.shape
    positions, hidden = slope.shape[2], slope.shape[3]
    return call(
        slope_kernel,
        [(1, LANES), (1, channels), (2, channels), (2, 2 * hidden), (positions, channels)],
        [VMEM] * 4 + [HBM, HBM, HBM, VMEM, HBM, VMEM, VMEM],
        [
            pltpu.VMEM(projection.shape, F32),
            pltpu.VMEM((1, channels), F32),
            pltpu.VMEM(down.shape, F32),
            pltpu.VMEM(up.shape, F32),
            pltpu.VMEM(packed.shape, F32),
            pltpu.SemaphoreType.DMA((4,)),
        ],
        mib=24,
        flops=12 * positions * channels * hidden,
        moved=4 * projection.size,
    )(packed, other, unit, inverse, projection, scale, down, down_sib, up, up_sib, slope)


def weight_kernel(own_ref, across_ref, slope_ref, grad_ref, out_ref, *, shard):
    width = out_ref.shape[1]
    lanes = slice(shard * width, (shard + 1) * width)
    out_ref[...] = dot(own_ref[...], slope_ref[0, shard] * grad_ref[0:1, lanes], HIGH, ((0,), (0,)))
    out_ref[...] += dot(across_ref[...], slope_ref[1, shard] * grad_ref[1:2, lanes], HIGH, ((0,), (0,)))


def weight_grad(own, across, slope, grad, shard):
    positions, channels = own.shape
    hidden = slope.shape[3]
    return call(
        functools.partial(weight_kernel, shard=shard),
        [(channels, hidden)],
        [VMEM] * 4,
        mib=24,
        flops=12 * positions * channels * hidden,
        moved=4 * channels * hidden,
    )(own, across, slope, grad)[0]


def last_kernel(
    own_ref, across_ref, slope_ref, grad_ref, moved_ref, hidden_ref, hidden_sib_ref, branch_ref, branch_sib_ref,
    up_out, down_out,
):
    width = up_out.shape[1]
    up_out[...] = moved_ref[...] + dot(
        own_ref[...], slope_ref[0, 0] * grad_ref[0:1, :width], HIGH, ((0,), (0,))
    )
    up_out[...] += dot(across_ref[...], slope_ref[1, 0] * grad_ref[1:2, :width], HIGH, ((0,), (0,)))
    down_out[...] = dot(hidden_ref[:, :width], branch_ref[...], HIGH, ((0,), (0,))) + dot(
        hidden_sib_ref[:, width:], branch_sib_ref[...], HIGH, ((0,), (0,))
    )


def last_grads(own, across, slope, grad, moved, hidden, hidden_sib, branch, branch_sib):
    positions, channels = own.shape
    width = slope.shape[3]
    return call(
        last_kernel,
        [(channels, width), (width, channels)],
        [VMEM] * 9,
        mib=24,
        flops=12 * positions * channels * width,
        moved=12 * channels * width,
    )(own, across, slope, grad, moved, hidden, hidden_sib, branch, branch_sib)


def back_kernel(
    other_ref, slope_ref, grad_ref, up_hbm, up_sib_ref, unit_ref, rstd_ref, w_hbm, gain_hbm, const_ref,
    out_ref, up_ref, w_ref, gain_ref, pad, slope, normed, sems,
):
    tiles, side = unit_ref.shape[0], unit_ref.shape[1]
    reach = w_ref.shape[0] // 2
    channels = tiles * LANES
    width = up_ref.shape[1]
    copies = fetch(((up_hbm, up_ref), (w_hbm, w_ref), (gain_hbm, gain_ref.at[0])), sems)
    pad[...] = jnp.zeros_like(pad)
    slope[...] = jnp.zeros_like(slope)
    for copy in copies:
        copy.wait()
    normed[...] = other_ref[...] + (
        dot(slope_ref[0, 0] * grad_ref[0:1, :width], up_ref[...], HIGH, ((1,), (1,)))
        + dot(slope_ref[0, 1] * grad_ref[0:1, width:], up_sib_ref[...], HIGH, ((1,), (1,)))
    )
    first = jnp.zeros((side, 16, LANES), F32)
    second = jnp.zeros((side, 16, LANES), F32)
    for tile in range(tiles):
        lanes = slice(tile * LANES, (tile + 1) * LANES)
        for h in range(side):
            slope[tile, h, 0:side, :] = normed[h * side : (h + 1) * side, lanes] * gain_ref[:, lanes]
        first = first + slope[tile]
        second = second + slope[tile] * unit_ref[tile]
    first = jnp.sum(first, axis=-1, keepdims=True) * (1.0 / channels)
    second = jnp.sum(second, axis=-1, keepdims=True) * (1.0 / channels)
    rstd = rstd_ref[...]
    for tile in range(tiles):
        grad = rstd * (slope[tile] - first - unit_ref[tile] * second)
        for h in range(side):
            pad[tile, reach + h, pl.ds(reach, side), :] = grad[h, :side]

    @pl.loop(0, tiles)
    def _(tile):
        low, high = convolve(pad, w_ref, tile, side, True)
        slope[tile, :, 0:8, :] = low
        slope[tile, :, 8:16, :] = high

    for tile in range(tiles):
        const = const_ref[:, tile * LANES : (tile + 1) * LANES]
        for h in range(side):
            out_ref[pl.ds(h * side * tiles + tile, side, stride=tiles), :] = (
                slope[tile, h, 0:side, :] + const
            )


def back(other, slope, grad, up, up_sib, unit, rstd, dw_kernel, norm_gain, const):
    tiles, side = unit.shape[0], unit.shape[1]
    taps = dw_kernel.shape[0]
    channels = tiles * LANES
    return call(
        back_kernel,
        [(side * side * tiles, LANES)],
        [VMEM, VMEM, VMEM, HBM, VMEM, VMEM, VMEM, HBM, HBM, VMEM],
        [
            pltpu.VMEM(up.shape, F32),
            pltpu.VMEM(dw_kernel.shape, F32),
            pltpu.VMEM((1, channels), F32),
            pltpu.VMEM((tiles, side + taps - 1, 24, LANES), F32),
            pltpu.VMEM((tiles, side, 16, LANES), F32),
            pltpu.VMEM((side * side, channels), F32),
            pltpu.SemaphoreType.DMA((3,)),
        ],
        mib=24,
        flops=side * side * channels * 2 * taps * taps,
        moved=12 * side * side * channels,
    )(other, slope, grad, up, up_sib, unit, rstd, dw_kernel, norm_gain, const)[0]


def column_kernel(images_ref, t0_ref, t1_ref, t2_ref, t3_ref, dp_ref, scale_ref, shift_ref, o0, o1, o2, o3):
    images = images_ref[...]
    for k, (text, out) in enumerate(((t0_ref, o0), (t1_ref, o1), (t2_ref, o2), (t3_ref, o3))):
        unit, _ = normal(text[...])
        logits = scale_ref[0] * jnp.sum(images * unit, axis=-1, keepdims=True) + shift_ref[0]
        slopes = 1.0 / (1.0 + jnp.exp(-logits))
        if k == 0:
            rows = lax.broadcasted_iota(jnp.int32, logits.shape, 0)
            slopes = slopes - jnp.where(rows == dp_ref[0], 1.0, 0.0)
        out[...] = jnp.sum(images * (scale_ref[0] * slopes), axis=0, keepdims=True)


def columns_of(images, texts, dp, scale, shift):
    return call(
        column_kernel,
        [texts[0].shape] * 4,
        [VMEM] * 5 + [SMEM] * 3,
        mib=8,
        flops=16 * images.size,
        moved=4 * images.size,
    )(images, *texts, dp, scale, shift)


def text_kernel(text_ref, a_ref, b_ref, c_ref, d_ref, out_ref):
    unit, inverse = normal(text_ref[...])
    step = a_ref[...] + b_ref[...] + (c_ref[...] + d_ref[...])
    out_ref[...] = inverse * (step - unit * jnp.sum(unit * step, axis=-1, keepdims=True))


def text_grads(text, parts):
    return call(text_kernel, [text.shape], [VMEM] * 5, mib=8)(text, *parts)[0]


def swapped(value, by):
    peers = lax.axis_size("fsdp")
    return lax.ppermute(value, "fsdp", [(i, i ^ by) for i in range(peers)])


def spread_out(rows):
    return lax.all_to_all(rows, "dp", 0, 0, tiled=True)


def body(
    images,
    dw_kernel,
    norm_gain,
    up_weight,
    up_bias,
    down_weight,
    layer_scale,
    projection,
    text_embed,
    logit_scale,
    logit_bias,
):
    dp = lax.axis_index("dp").astype(jnp.int32)[None]
    scale, shift = logit_scale[None], logit_bias[None]
    up_sib, down_sib, bias_sib = swapped(up_weight, 1), swapped(down_weight, 1), swapped(up_bias, 1)
    group_texts = (text_embed,) + tuple(swapped(text_embed, k) for k in (1, 2, 3))

    normed, unit, rstd, image_sum = front(images, dw_kernel, norm_gain)
    across = swapped(normed, 2)
    texts = spread_out(jnp.broadcast_to(text_embed, (lax.axis_size("dp"), text_embed.shape[1])))
    texts_sib = swapped(texts, 1)
    slope, hidden, part = mlp(
        normed, across, up_weight, up_sib, up_bias, bias_sib, down_weight, down_sib, layer_scale, image_sum
    )
    image_unit, spread, inverse, packed = pairs(
        part, swapped(part, 2), projection, texts, texts_sib, dp, scale, shift
    )
    losses, const, branch, grad, across_grad = slopes_of(
        packed, swapped(packed, 2), image_unit, inverse, projection, layer_scale,
        down_weight, down_sib, up_weight, up_sib, slope,
    )
    other_grad = swapped(across_grad, 2)
    moved = swapped(weight_grad(normed, across, slope, grad, 1), 1)
    image_units = spread_out(spread)
    input_grad = back(
        other_grad, slope, grad, up_weight, up_sib, unit, rstd, dw_kernel, norm_gain, const
    )
    steps = columns_of(image_units, group_texts, dp, scale, shift)
    up_grad, down_grad = last_grads(
        normed, across, slope, grad, moved, hidden, swapped(hidden, 1), branch, swapped(branch, 1)
    )
    text_grad = text_grads(
        text_embed, (steps[0],) + tuple(swapped(steps[k], k) for k in (1, 2, 3))
    )
    return (
        input_grad.reshape(images.shape),
        up_grad[None],
        down_grad[None],
        text_grad,
        losses[0, :1],
    )


def solution(mesh):
    placed = (
        P(("dp", "fsdp"), None, None, None),
        P(),
        P(),
        P(None, "fsdp"),
        P("fsdp"),
        P("fsdp", None),
        P(),
        P(),
        P(("dp", "fsdp"), None),
        P(),
        P(),
    )
    return jax.shard_map(
        body,
        mesh=mesh,
        in_specs=placed,
        out_specs=(
            P(("dp", "fsdp"), None, None, None),
            P("dp", None, "fsdp"),
            P("dp", "fsdp", None),
            P(("dp", "fsdp"), None),
            P(("dp", "fsdp")),
        ),
        check_vma=False,
    )
```

```python
import functools

import jax
import jax.numpy as jnp
from jax import lax
from jax.experimental import pallas as pl
from jax.experimental.pallas import tpu as pltpu
from jax.sharding import PartitionSpec as P

LANES = 128
HIGH = lax.Precision.HIGH
VMEM = pl.BlockSpec(memory_space=pltpu.VMEM)
SMEM = pl.BlockSpec(memory_space=pltpu.SMEM)
ANY = pl.BlockSpec(memory_space=pl.ANY)
F32 = jnp.float32
WIDE = 58


def call(kernel, outs, specs, scratch=(), us=1.0, mib=12):
    return pl.pallas_call(
        kernel,
        out_shape=[jax.ShapeDtypeStruct(shape, F32) for shape in outs],
        in_specs=specs,
        out_specs=[VMEM] * len(outs),
        scratch_shapes=list(scratch),
        compiler_params=pltpu.CompilerParams(vmem_limit_bytes=mib << 20),
        cost_estimate=pl.CostEstimate(
            flops=int(us * 1.15e9), bytes_accessed=int(us * 3.0e6), transcendentals=0
        ),
    )


def fetch(sems, *pairs):
    copies = [
        pltpu.make_async_copy(source, target, sems.at[i])
        for i, (source, target) in enumerate(pairs)
    ]
    for copy in copies:
        copy.start()
    return copies


def dot(left, right, dims=((1,), (0,))):
    return lax.dot_general(
        left, right, (dims, ((), ())), precision=HIGH, preferred_element_type=F32
    )


def row_dots(matrix_ref, vectors):
    count, width = matrix_ref.shape
    rows = [[] for _ in vectors]
    for block in range(count // LANES):
        for i, vector in enumerate(vectors):
            total = jnp.zeros((LANES, LANES), F32)
            for tile in range(width // LANES):
                lanes = slice(tile * LANES, (tile + 1) * LANES)
                total = total + matrix_ref[block * LANES : (block + 1) * LANES, lanes] * vector[:, lanes]
            rows[i].append(jnp.sum(total.T, axis=0, keepdims=True))
    return [jnp.concatenate(row, axis=1) for row in rows]


def gathered_rows(flat_ref, rows_ref):
    tiles = rows_ref.shape[1] // LANES
    count = rows_ref.shape[0]
    for tile in range(tiles):
        rows_ref[:, tile * LANES : (tile + 1) * LANES] = flat_ref[pl.ds(tile, count, stride=tiles), :]


def lanes_of(tile):
    return pl.ds(pl.multiple_of(tile * LANES, LANES), LANES)


def convolve(pad, w_ref, tile, side, flip):
    taps = w_ref.shape[0]
    halves = []
    for half in range(2):
        total = jnp.zeros((side, 8, LANES), F32)
        for q in range(taps):
            column = pad[tile, :, pl.ds(q + 8 * half, 8), :]
            for p in range(taps):
                row = taps - 1 - p if flip else p
                col = taps - 1 - q if flip else q
                total = total + column[p : p + side] * w_ref[row, pl.ds(col, 1), lanes_of(tile)]
        halves.append(total)
    return halves


def front_kernel(
    x_any, w_any, gain_any, normed_ref, rstd_ref, sum_ref, gain_ref, x_ref, w_ref, pad, mixed, sems
):
    tiles, side = mixed.shape[0], mixed.shape[1]
    reach = w_ref.shape[0] // 2
    channels = tiles * LANES
    copies = fetch(sems, (x_any, x_ref), (w_any, w_ref), (gain_any, gain_ref.at[0]))
    pad[...] = jnp.zeros_like(pad)
    for copy in copies:
        copy.wait()
    for tile in range(tiles):
        total = jnp.zeros((side, LANES), F32)
        for h in range(side):
            row = x_ref[pl.ds(h * side * tiles + tile, side, stride=tiles), :]
            pad[tile, reach + h, pl.ds(reach, side), :] = row
            total = total + row
        sum_ref[:, tile * LANES : (tile + 1) * LANES] = jnp.sum(total, axis=0, keepdims=True)

    @pl.loop(0, tiles)
    def _(tile):
        low, high = convolve(pad, w_ref, tile, side, False)
        mixed[tile, :, 0:8, :] = low
        mixed[tile, :, 8:16, :] = high

    total = mixed[0]
    for tile in range(1, tiles):
        total = total + mixed[tile]
    mean = jnp.sum(total, axis=-1, keepdims=True) * (1.0 / channels)
    square = jnp.zeros((side, 16, LANES), F32)
    for tile in range(tiles):
        off = mixed[tile] - mean
        square = square + off * off
    rstd = lax.rsqrt(jnp.sum(square, axis=-1, keepdims=True) * (1.0 / channels) + 1e-06)
    rstd_ref[...] = jnp.broadcast_to(rstd, rstd_ref.shape)
    for tile in range(tiles):
        lanes = slice(tile * LANES, (tile + 1) * LANES)
        out = (mixed[tile] - mean) * rstd * gain_ref[:, lanes]
        for h in range(side):
            normed_ref[h * side : (h + 1) * side, lanes] = out[h, :side]
    rest = normed_ref.shape[0] - side * side
    normed_ref[side * side :, :] = jnp.zeros((rest, channels), F32)


def front(images, dw_kernel, norm_gain):
    side, taps = images.shape[1], dw_kernel.shape[0]
    channels = images.shape[3]
    tiles = channels // LANES
    return call(
        front_kernel,
        [
            (pl.cdiv(side * side, 8) * 8, channels),
            (side, 16, LANES),
            (1, channels),
            (1, channels),
        ],
        [ANY] * 3,
        [
            pltpu.VMEM((side * side * tiles, LANES), F32),
            pltpu.VMEM(dw_kernel.shape, F32),
            pltpu.VMEM((tiles, side + taps - 1, 24, LANES), F32),
            pltpu.VMEM((tiles, side, 16, LANES), F32),
            pltpu.SemaphoreType.DMA((3,)),
        ],
        us=4.0,
        mib=WIDE,
    )(images.reshape(-1, LANES), dw_kernel, norm_gain)


def spread_kernel(row_ref, other_ref, out_ref):
    tiles = row_ref.shape[1] // LANES
    copies = out_ref.shape[0] // (2 * tiles)
    for k, row in enumerate((row_ref, other_ref)):
        for tile in range(tiles):
            out_ref[pl.ds(k * tiles + tile, copies, stride=2 * tiles), :] = jnp.broadcast_to(
                row[0:1, tile * LANES : (tile + 1) * LANES], (copies, LANES)
            )


def spread_pair(row, other, peers):
    flat = (peers * row.shape[1] // LANES, LANES)
    return call(spread_kernel, [flat], [VMEM] * 2, us=0.5)(row, other)[0]


def mlp_kernel(
    own_any, across_any, up_any, up_sib_any, bias_any, bias_sib_any, down_any, down_sib_any, scale_any, proj_any,
    sum_any, both_ref, slope_ref, slope_sib_ref, hidden_ref, part_ref,
    up_ref, up_sib_ref, bias_ref, down_ref, down_sib_ref, scale_ref, proj_ref, sum_ref, sems, *, positions,
):
    offset = own_any.shape[0]
    width = up_ref.shape[1]
    copies = fetch(
        sems,
        (own_any, both_ref.at[pl.ds(0, offset)]),
        (across_any, both_ref.at[pl.ds(offset, offset)]),
        (up_any, up_ref),
        (bias_any, bias_ref.at[0]),
        (bias_sib_any, bias_ref.at[1]),
        (up_sib_any, up_sib_ref),
        (scale_any, scale_ref.at[0]),
        (sum_any, sum_ref),
        (down_any, down_ref),
        (down_sib_any, down_sib_ref),
        (proj_any, proj_ref),
    )
    for copy in copies[:5]:
        copy.wait()
    for s, (weight, out) in enumerate(((up_ref, slope_ref), (up_sib_ref, slope_sib_ref))):
        if s == 1:
            copies[5].wait()
        pre = dot(both_ref[...], weight[...]) + bias_ref[pl.ds(s, 1), :]
        cdf = 0.5 * (1.0 + lax.erf(pre * (0.5**0.5)))
        out[...] = cdf + pre * (jnp.exp(-0.5 * pre * pre) * 0.3989422804014327)
        act = pre * cdf
        for k in range(2):
            hidden_ref[pl.ds(k, 1), s * width : (s + 1) * width] = jnp.sum(
                act[k * offset : k * offset + positions], axis=0, keepdims=True
            )
    hidden = hidden_ref[...]
    for copy in copies[6:10]:
        copy.wait()
    part = dot(hidden[:, :width], down_ref[...]) + dot(hidden[:, width:], down_sib_ref[...])
    part = part * scale_ref[...]
    own = lax.broadcasted_iota(jnp.int32, part.shape, 0) == 0
    part = part + jnp.where(own, sum_ref[...], 0.0)
    copies[10].wait()
    part_ref[...] = dot(part * (1.0 / positions), proj_ref[...])


def mlp(own, across, up, up_sib, bias, bias_sib, down, down_sib, scale, projection, image_sum, positions):
    channels = own.shape[1]
    hidden = up.shape[1]
    rows = 2 * own.shape[0]
    return call(
        functools.partial(mlp_kernel, positions=positions),
        [
            (rows, channels), (rows, hidden), (rows, hidden), (2, 2 * hidden),
            (2, projection.shape[1]),
        ],
        [ANY] * 11,
        [
            pltpu.VMEM(up.shape, F32),
            pltpu.VMEM(up.shape, F32),
            pltpu.VMEM((2, hidden), F32),
            pltpu.VMEM(down.shape, F32),
            pltpu.VMEM(down.shape, F32),
            pltpu.VMEM((1, channels), F32),
            pltpu.VMEM(projection.shape, F32),
            pltpu.VMEM(image_sum.shape, F32),
            pltpu.SemaphoreType.DMA((11,)),
        ],
        us=5.0,
        mib=WIDE,
    )(own, across, up, up_sib, bias, bias_sib, down, down_sib, scale, projection, image_sum)


def normal(rows):
    inverse = lax.rsqrt(jnp.sum(rows * rows, axis=-1, keepdims=True) + 1e-06)
    return rows * inverse, inverse


def pair_kernel(
    mine_ref, other_ref, texts_ref, texts_sib_ref, dp_ref, scale_ref, shift_ref,
    unit_ref, inverse_ref, packed_ref, features, text, text_sib,
):
    embed = unit_ref.shape[1]
    gathered_rows(texts_ref, text)
    gathered_rows(texts_sib_ref, text_sib)
    features[pl.ds(0, 1), :] = mine_ref[pl.ds(0, 1), :] + other_ref[pl.ds(1, 1), :]
    features[pl.ds(1, 1), :] = mine_ref[pl.ds(1, 1), :] + other_ref[pl.ds(0, 1), :]
    unit, inverse = normal(features[...])
    inverse_ref[...] = jnp.broadcast_to(inverse, inverse_ref.shape)
    unit_ref[...] = unit
    step = jnp.zeros(unit.shape, F32)
    losses = jnp.zeros((2, 1), F32)
    for s, block_ref in enumerate((text, text_sib)):
        block, _ = normal(block_ref[...])
        logits = scale_ref[0] * dot(unit, block, ((1,), (1,))) + shift_ref[0]
        if s == 0:
            columns = lax.broadcasted_iota(jnp.int32, logits.shape, 1)
            place = lax.broadcasted_iota(jnp.int32, logits.shape, 0)
            match = jnp.where((place == 0) & (columns == dp_ref[0]), 1.0, 0.0)
        else:
            match = jnp.zeros(logits.shape, F32)
        flipped = (1.0 - 2.0 * match) * logits
        tail = jnp.log1p(jnp.exp(-jnp.abs(flipped)))
        losses = losses + jnp.sum(jnp.maximum(flipped, 0.0) + tail, axis=1, keepdims=True)
        slopes = 1.0 / (1.0 + jnp.exp(-logits)) - match
        step = step + dot(slopes, block)
    packed_ref[:, :embed] = step * scale_ref[0]
    packed_ref[:, embed:] = jnp.broadcast_to(losses, (2, LANES))


def pairs(mine, other, texts, texts_sib, dp, scale, shift):
    embed = mine.shape[1]
    count = texts.size // embed
    return call(
        pair_kernel,
        [(2, embed), (2, LANES), (2, embed + LANES)],
        [VMEM] * 4 + [SMEM] * 3,
        [
            pltpu.VMEM(mine.shape, F32),
            pltpu.VMEM((count, embed), F32),
            pltpu.VMEM((count, embed), F32),
        ],
        us=6.0,
    )(mine, other, texts, texts_sib, dp, scale, shift)


def scaled(slope_ref, rows):
    second = lax.broadcasted_iota(jnp.int32, slope_ref.shape, 0) >= slope_ref.shape[0] // 2
    return slope_ref[...] * jnp.where(second, rows[1:2], rows[0:1])


def slope_kernel(
    packed_ref, other_ref, unit_ref, inverse_ref, proj_ref, scale_ref, down_ref, down_sib_ref, up_ref, up_sib_ref,
    slope_ref, slope_sib_ref, loss_ref, const_ref, grad_ref, own_ref, across_ref, sums,
):
    embed = unit_ref.shape[1]
    width = down_ref.shape[0]
    positions = own_ref.shape[0]
    offset = slope_ref.shape[0] // 2
    sums[pl.ds(0, 1), :] = packed_ref[pl.ds(0, 1), :] + other_ref[pl.ds(1, 1), :]
    sums[pl.ds(1, 1), :] = packed_ref[pl.ds(1, 1), :] + other_ref[pl.ds(0, 1), :]
    loss_ref[...] = sums[0:1, embed:]
    step, unit = sums[:, :embed], unit_ref[...]
    grad = step - unit * jnp.sum(unit * step, axis=-1, keepdims=True)
    grad = grad * (inverse_ref[:, 0:1] * (1.0 / positions))
    rows = row_dots(proj_ref, (grad[0:1], grad[1:2]))
    const_ref[...] = rows[0]
    for k in range(2):
        grad_ref[pl.ds(2 + k, 1), :] = rows[k] * scale_ref[...]
    branch = grad_ref[2:4, :]
    for s, weight in enumerate((down_ref, down_sib_ref)):
        for k, row in enumerate(row_dots(weight, (branch[0:1], branch[1:2]))):
            grad_ref[pl.ds(k, 1), s * width : (s + 1) * width] = row
    rows = grad_ref[...]
    total = dot(scaled(slope_ref, rows[:, :width]), up_ref[...], ((1,), (1,)))
    total = total + dot(scaled(slope_sib_ref, rows[:, width:]), up_sib_ref[...], ((1,), (1,)))
    own_ref[...] = total[:positions]
    across_ref[...] = total[offset : offset + positions]


def slopes_of(packed, other, unit, inverse, projection, scale, down, down_sib, up, up_sib, slope, slope_sib, positions):
    channels = up.shape[0]
    return call(
        slope_kernel,
        [(1, LANES), (1, channels), (4, channels), (positions, channels), (positions, channels)],
        [VMEM] * 12,
        [pltpu.VMEM(packed.shape, F32)],
        us=4.0,
        mib=16,
    )(packed, other, unit, inverse, projection, scale[None], down, down_sib, up, up_sib, slope, slope_sib)


def last_kernel(
    both_ref, both_sib_ref, slope_ref, slope_sib_ref, grad_ref, grad_sib_ref, hidden_ref, hidden_sib_ref,
    up_out, down_out,
):
    width = up_out.shape[1]
    rows, rows_sib = grad_ref[...], grad_sib_ref[...]
    up_out[...] = dot(both_ref[...], scaled(slope_ref, rows[:, :width]), ((0,), (0,)))
    up_out[...] += dot(both_sib_ref[...], scaled(slope_sib_ref, rows_sib[:, width:]), ((0,), (0,)))
    down_out[...] = dot(hidden_ref[:, :width], rows[2:4], ((0,), (0,))) + dot(
        hidden_sib_ref[:, width:], rows_sib[2:4], ((0,), (0,))
    )


def last_grads(both, both_sib, slope, slope_sib, grad, grad_sib, hidden, hidden_sib):
    channels, width = both.shape[1], slope.shape[1]
    return call(
        last_kernel, [(channels, width), (width, channels)], [VMEM] * 8, us=0.2, mib=16
    )(both, both_sib, slope, slope_sib, grad, grad_sib, hidden, hidden_sib)


def back_kernel(
    mine_ref, other_ref, both_ref, rstd_ref, w_ref, gain_ref, const_ref, out_ref, pad, slope, unit
):
    tiles, side = slope.shape[0], slope.shape[1]
    reach = w_ref.shape[0] // 2
    channels = tiles * LANES
    pad[...] = jnp.zeros_like(pad)
    unit[...] = jnp.zeros_like(unit)
    slope[...] = jnp.zeros_like(slope)
    first = jnp.zeros((side, 16, LANES), F32)
    second = jnp.zeros((side, 16, LANES), F32)
    for tile in range(tiles):
        lanes = slice(tile * LANES, (tile + 1) * LANES)
        invert = 1.0 / gain_ref[:, lanes]
        for h in range(side):
            rows = slice(h * side, (h + 1) * side)
            unit[tile, h, 0:side, :] = both_ref[rows, lanes] * invert
            slope[tile, h, 0:side, :] = (mine_ref[rows, lanes] + other_ref[rows, lanes]) * gain_ref[:, lanes]
        first = first + slope[tile]
        second = second + slope[tile] * unit[tile]
    first = jnp.sum(first, axis=-1, keepdims=True) * (1.0 / channels)
    second = jnp.sum(second, axis=-1, keepdims=True) * (1.0 / channels)
    rstd = rstd_ref[...]
    for tile in range(tiles):
        grad = rstd * (slope[tile] - first - unit[tile] * second)
        for h in range(side):
            pad[tile, reach + h, pl.ds(reach, side), :] = grad[h, :side]

    @pl.loop(0, tiles)
    def _(tile):
        low, high = convolve(pad, w_ref, tile, side, True)
        slope[tile, :, 0:8, :] = low
        slope[tile, :, 8:16, :] = high

    for tile in range(tiles):
        const = const_ref[:, tile * LANES : (tile + 1) * LANES]
        for h in range(side):
            out_ref[pl.ds(h * side * tiles + tile, side, stride=tiles), :] = (
                slope[tile, h, 0:side, :] + const
            )


def back(mine, other, both, rstd, dw_kernel, norm_gain, const, side):
    taps, channels = dw_kernel.shape[0], dw_kernel.shape[2]
    tiles = channels // LANES
    return call(
        back_kernel,
        [(side * side * tiles, LANES)],
        [VMEM] * 7,
        [
            pltpu.VMEM((tiles, side + taps - 1, 24, LANES), F32),
            pltpu.VMEM((tiles, side, 16, LANES), F32),
            pltpu.VMEM((tiles, side, 16, LANES), F32),
        ],
        us=4.0,
    )(mine, other, both, rstd, dw_kernel, norm_gain, const)[0]


def column_kernel(
    flat_ref, t0_ref, t1_ref, t2_ref, t3_ref, dp_ref, scale_ref, shift_ref, o0, o1, o2, o3, images_ref
):
    gathered_rows(flat_ref, images_ref)
    images = images_ref[...]
    for k, (text, out) in enumerate(((t0_ref, o0), (t1_ref, o1), (t2_ref, o2), (t3_ref, o3))):
        unit, _ = normal(text[...])
        logits = scale_ref[0] * jnp.sum(images * unit, axis=-1, keepdims=True) + shift_ref[0]
        slopes = 1.0 / (1.0 + jnp.exp(-logits))
        if k == 0:
            rows = lax.broadcasted_iota(jnp.int32, logits.shape, 0)
            slopes = slopes - jnp.where(rows == dp_ref[0], 1.0, 0.0)
        out[...] = jnp.sum(images * (scale_ref[0] * slopes), axis=0, keepdims=True)


def columns_of(images, texts, dp, scale, shift):
    embed = texts[0].shape[1]
    return call(
        column_kernel,
        [texts[0].shape] * 4,
        [VMEM] * 5 + [SMEM] * 3,
        [pltpu.VMEM((images.size // embed, embed), F32)],
        us=0.5,
    )(images, *texts, dp, scale, shift)


def text_kernel(text_ref, a_ref, b_ref, c_ref, d_ref, out_ref):
    unit, inverse = normal(text_ref[...])
    step = a_ref[...] + b_ref[...] + (c_ref[...] + d_ref[...])
    out_ref[...] = inverse * (step - unit * jnp.sum(unit * step, axis=-1, keepdims=True))


def text_grads(text, parts):
    return call(text_kernel, [text.shape], [VMEM] * 5, us=0.5)(text, *parts)[0]


def swapped(value, by):
    peers = lax.axis_size("fsdp")
    return lax.ppermute(value, "fsdp", [(i, i ^ by) for i in range(peers)])


def mirrored(value):
    peers = lax.axis_size("dp")
    return lax.ppermute(value, "dp", [(i, i ^ 1) for i in range(peers)])


def spread_out(flat):
    peers = lax.axis_size("dp")
    groups = [list(range(start, peers, 2)) for start in range(2)]
    rows = flat.reshape(peers // 2, 1, -1)
    return lax.all_to_all(
        rows, "dp", 0, 0, axis_index_groups=groups, tiled=True
    ).reshape(flat.shape)


def body(
    images,
    dw_kernel,
    norm_gain,
    up_weight,
    up_bias,
    down_weight,
    layer_scale,
    projection,
    text_embed,
    logit_scale,
    logit_bias,
):
    positions = images.shape[1] * images.shape[2]
    peers = lax.axis_size("dp")
    place = (lax.axis_index("dp") // 2 * 2).astype(jnp.int32)[None]
    scale, shift = logit_scale[None], logit_bias[None]
    text_other = mirrored(text_embed)
    up_sib, down_sib, bias_sib = swapped(up_weight, 1), swapped(down_weight, 1), swapped(up_bias, 1)

    normed, rstd, image_sum, gain = front(images, dw_kernel, norm_gain)
    text_other, normed = lax.optimization_barrier((text_other, normed))
    across = swapped(normed, 2)
    texts = spread_out(spread_pair(text_embed, text_other, peers))
    group_texts = tuple(swapped(text_embed, k) for k in (1, 2, 3))
    across, group_texts = lax.optimization_barrier((across, group_texts))
    both, slope, slope_sib, hidden, part = mlp(
        normed, across, up_weight, up_sib, up_bias, bias_sib, down_weight, down_sib, layer_scale,
        projection, image_sum, images.shape[1] * images.shape[2],
    )
    part_other = swapped(part, 2)
    texts, hidden = lax.optimization_barrier((texts, hidden))
    texts_sib = swapped(texts, 1)
    image_unit, inverse, packed = pairs(
        part, part_other, texts, texts_sib, place, scale, shift
    )
    packed_other = swapped(packed, 2)
    unit_other = mirrored(image_unit)
    packed_other, unit_other = lax.optimization_barrier((packed_other, unit_other))
    losses, const, grad, own_grad, across_grad = slopes_of(
        packed, packed_other, image_unit, inverse, projection, layer_scale,
        down_weight, down_sib, up_weight, up_sib, slope, slope_sib, images.shape[1] * images.shape[2],
    )
    grad, both, slope_sib, hidden = lax.optimization_barrier((grad, both, slope_sib, hidden))
    both_sib, slope_back, hidden_sib = swapped(both, 1), swapped(slope_sib, 1), swapped(hidden, 1)
    across_grad, image_unit, unit_other = lax.optimization_barrier((across_grad, image_unit, unit_other))
    other_grad = swapped(across_grad, 2)
    image_units = spread_out(spread_pair(image_unit, unit_other, peers))
    up_grad, down_grad = last_grads(
        both, both_sib, slope, slope_back, grad, swapped(grad, 1), hidden, hidden_sib
    )
    image_units, up_grad = lax.optimization_barrier((image_units, up_grad))
    steps = columns_of(image_units, (text_embed,) + group_texts, place, scale, shift)
    input_grad = back(own_grad, other_grad, both, rstd, dw_kernel, gain, const, images.shape[1])
    first_step, input_grad = lax.optimization_barrier((steps[0], input_grad))
    text_grad = text_grads(
        text_embed, (first_step,) + tuple(swapped(steps[k], k) for k in (1, 2, 3))
    )
    return (
        input_grad.reshape(images.shape),
        up_grad[None],
        down_grad[None],
        text_grad,
        losses[0, :1],
    )


def solution(mesh):
    placed = (
        P(("dp", "fsdp"), None, None, None),
        P(),
        P(),
        P(None, "fsdp"),
        P("fsdp"),
        P("fsdp", None),
        P(),
        P(),
        P(("dp", "fsdp"), None),
        P(),
        P(),
    )
    return jax.shard_map(
        body,
        mesh=mesh,
        in_specs=placed,
        out_specs=(
            P(("dp", "fsdp"), None, None, None),
            P("dp", None, "fsdp"),
            P("dp", "fsdp", None),
            P(("dp", "fsdp"), None),
            P(("dp", "fsdp")),
        ),
        check_vma=False,
    )
```

```python
import functools

import jax
import jax.numpy as jnp
from jax import lax
from jax.experimental import pallas as pl
from jax.experimental.pallas import tpu as pltpu
from jax.sharding import PartitionSpec as P

LANES = 128
HIGH = lax.Precision.HIGH
VMEM = pl.BlockSpec(memory_space=pltpu.VMEM)
SMEM = pl.BlockSpec(memory_space=pltpu.SMEM)
ANY = pl.BlockSpec(memory_space=pl.ANY)
F32 = jnp.float32
WIDE = 58


def call(kernel, outs, specs, scratch=(), us=1.0, mib=12):
    return pl.pallas_call(
        kernel,
        out_shape=[jax.ShapeDtypeStruct(shape, F32) for shape in outs],
        in_specs=specs,
        out_specs=[VMEM] * len(outs),
        scratch_shapes=list(scratch),
        compiler_params=pltpu.CompilerParams(vmem_limit_bytes=mib << 20),
        cost_estimate=pl.CostEstimate(
            flops=int(us * 1.15e9), bytes_accessed=int(us * 3.0e6), transcendentals=0
        ),
    )


def fetch(sems, *pairs):
    copies = [
        pltpu.make_async_copy(source, target, sems.at[i])
        for i, (source, target) in enumerate(pairs)
    ]
    for copy in copies:
        copy.start()
    return copies


def dot(left, right, dims=((1,), (0,))):
    return lax.dot_general(
        left, right, (dims, ((), ())), precision=HIGH, preferred_element_type=F32
    )


def row_dots(matrix_ref, vectors):
    count, width = matrix_ref.shape
    rows = [[] for _ in vectors]
    for block in range(count // LANES):
        for i, vector in enumerate(vectors):
            total = jnp.zeros((LANES, LANES), F32)
            for tile in range(width // LANES):
                lanes = slice(tile * LANES, (tile + 1) * LANES)
                total = total + matrix_ref[block * LANES : (block + 1) * LANES, lanes] * vector[:, lanes]
            rows[i].append(jnp.sum(total.T, axis=0, keepdims=True))
    return [jnp.concatenate(row, axis=1) for row in rows]


def column_dots(vectors, matrix_ref):
    count, width = matrix_ref.shape
    totals = [[None] * (width // LANES) for _ in vectors]
    for block in range(count // LANES):
        rows = slice(block * LANES, (block + 1) * LANES)
        for i, vector in enumerate(vectors):
            column = jnp.broadcast_to(vector[:, rows], (LANES, LANES)).T
            for tile in range(width // LANES):
                term = matrix_ref[rows, tile * LANES : (tile + 1) * LANES] * column
                term = jnp.sum(term.reshape(LANES // 8, 8, LANES), axis=0)
                old = totals[i][tile]
                totals[i][tile] = term if old is None else old + term
    return [
        jnp.concatenate([jnp.sum(part, axis=0, keepdims=True) for part in total], axis=1)
        for total in totals
    ]


def gathered_rows(flat_ref, rows_ref):
    tiles = rows_ref.shape[1] // LANES
    count = rows_ref.shape[0]
    for tile in range(tiles):
        rows_ref[:, tile * LANES : (tile + 1) * LANES] = flat_ref[pl.ds(tile, count, stride=tiles), :]


def lanes_of(tile):
    return pl.ds(pl.multiple_of(tile * LANES, LANES), LANES)


def convolve(pad, w_ref, tile, side, flip):
    taps = w_ref.shape[0]
    halves = []
    for half in range(2):
        total = jnp.zeros((side, 8, LANES), F32)
        for q in range(taps):
            column = pad[tile, :, pl.ds(q + 8 * half, 8), :]
            for p in range(taps):
                row = taps - 1 - p if flip else p
                col = taps - 1 - q if flip else q
                total = total + column[p : p + side] * w_ref[row, pl.ds(col, 1), lanes_of(tile)]
        halves.append(total)
    return halves


def front_kernel(
    x_any, w_any, gain_any, normed_ref, rstd_ref, sum_ref, gain_ref, x_ref, w_ref, pad, mixed, sems
):
    tiles, side = mixed.shape[0], mixed.shape[1]
    reach = w_ref.shape[0] // 2
    channels = tiles * LANES
    copies = fetch(sems, (x_any, x_ref), (w_any, w_ref), (gain_any, gain_ref.at[0]))
    pad[...] = jnp.zeros_like(pad)
    for copy in copies:
        copy.wait()
    for tile in range(tiles):
        total = jnp.zeros((side, LANES), F32)
        for h in range(side):
            row = x_ref[pl.ds(h * side * tiles + tile, side, stride=tiles), :]
            pad[tile, reach + h, pl.ds(reach, side), :] = row
            total = total + row
        sum_ref[:, tile * LANES : (tile + 1) * LANES] = jnp.sum(total, axis=0, keepdims=True)

    @pl.loop(0, tiles)
    def _(tile):
        low, high = convolve(pad, w_ref, tile, side, False)
        mixed[tile, :, 0:8, :] = low
        mixed[tile, :, 8:16, :] = high

    total = mixed[0]
    for tile in range(1, tiles):
        total = total + mixed[tile]
    mean = jnp.sum(total, axis=-1, keepdims=True) * (1.0 / channels)
    square = jnp.zeros((side, 16, LANES), F32)
    for tile in range(tiles):
        off = mixed[tile] - mean
        square = square + off * off
    rstd = lax.rsqrt(jnp.sum(square, axis=-1, keepdims=True) * (1.0 / channels) + 1e-06)
    rstd_ref[...] = jnp.broadcast_to(rstd, rstd_ref.shape)
    for tile in range(tiles):
        lanes = slice(tile * LANES, (tile + 1) * LANES)
        out = (mixed[tile] - mean) * rstd * gain_ref[:, lanes]
        for h in range(side):
            normed_ref[h * side : (h + 1) * side, lanes] = out[h, :side]
    rest = normed_ref.shape[0] - side * side
    normed_ref[side * side :, :] = jnp.zeros((rest, channels), F32)


def front(images, dw_kernel, norm_gain):
    side, taps = images.shape[1], dw_kernel.shape[0]
    channels = images.shape[3]
    tiles = channels // LANES
    return call(
        front_kernel,
        [
            (pl.cdiv(side * side, 8) * 8, channels),
            (side, 16, LANES),
            (1, channels),
            (1, channels),
        ],
        [ANY] * 3,
        [
            pltpu.VMEM((side * side * tiles, LANES), F32),
            pltpu.VMEM(dw_kernel.shape, F32),
            pltpu.VMEM((tiles, side + taps - 1, 24, LANES), F32),
            pltpu.VMEM((tiles, side, 16, LANES), F32),
            pltpu.SemaphoreType.DMA((3,)),
        ],
        us=4.0,
        mib=WIDE,
    )(images.reshape(-1, LANES), dw_kernel, norm_gain)


def spread_rows(row, out_ref, place):
    tiles = row.shape[1] // LANES
    copies = out_ref.shape[0] // (2 * tiles)
    for tile in range(tiles):
        out_ref[pl.ds(place * tiles + tile, copies, stride=2 * tiles), :] = jnp.broadcast_to(
            row[:, tile * LANES : (tile + 1) * LANES], (copies, LANES)
        )


def spread_kernel(row_ref, other_ref, out_ref):
    spread_rows(row_ref[...], out_ref, 0)
    spread_rows(other_ref[...], out_ref, 1)


def spread_pair(row, other, peers):
    flat = (peers * row.shape[1] // LANES, LANES)
    return call(spread_kernel, [flat], [VMEM] * 2, us=0.5)(row, other)[0]


def mlp_kernel(
    own_any, across_any, up_any, up_sib_any, bias_any, bias_sib_any, down_any, down_sib_any, scale_any, proj_any,
    sum_any, both_ref, slope_ref, slope_sib_ref, hidden_ref, part_ref,
    up_ref, up_sib_ref, bias_ref, down_ref, down_sib_ref, scale_ref, proj_ref, sum_ref, sems, late_sems,
    *, positions,
):
    offset = own_any.shape[0]
    width = up_ref.shape[1]
    copies = fetch(
        sems,
        (own_any, both_ref.at[pl.ds(0, offset)]),
        (across_any, both_ref.at[pl.ds(offset, offset)]),
        (up_any, up_ref),
        (bias_any, bias_ref.at[0]),
        (bias_sib_any, bias_ref.at[1]),
        (up_sib_any, up_sib_ref),
    )
    for copy in copies[:5]:
        copy.wait()
    late = fetch(
        late_sems,
        (scale_any, scale_ref.at[0]),
        (sum_any, sum_ref),
        (down_any, down_ref),
        (down_sib_any, down_sib_ref),
        (proj_any, proj_ref),
    )
    for s, (weight, out) in enumerate(((up_ref, slope_ref), (up_sib_ref, slope_sib_ref))):
        if s == 1:
            copies[5].wait()
        pre = dot(both_ref[...], weight[...]) + bias_ref[pl.ds(s, 1), :]
        cdf = 0.5 * (1.0 + lax.erf(pre * (0.5**0.5)))
        out[...] = cdf + pre * (jnp.exp(-0.5 * pre * pre) * 0.3989422804014327)
        act = pre * cdf
        for k in range(2):
            hidden_ref[pl.ds(k, 1), s * width : (s + 1) * width] = jnp.sum(
                act[k * offset : k * offset + positions], axis=0, keepdims=True
            )
    hidden = hidden_ref[...]
    for copy in late[:4]:
        copy.wait()
    first = column_dots((hidden[0:1, :width], hidden[1:2, :width]), down_ref)
    second = column_dots((hidden[0:1, width:], hidden[1:2, width:]), down_sib_ref)
    pooled = []
    for k in range(2):
        row = (first[k] + second[k]) * scale_ref[...]
        pooled.append((row + sum_ref[...] if k == 0 else row) * (1.0 / positions))
    late[4].wait()
    for k, row in enumerate(column_dots(pooled, proj_ref)):
        part_ref[pl.ds(k, 1), :] = row


def mlp(own, across, up, up_sib, bias, bias_sib, down, down_sib, scale, projection, image_sum, positions):
    channels = own.shape[1]
    hidden = up.shape[1]
    rows = 2 * own.shape[0]
    return call(
        functools.partial(mlp_kernel, positions=positions),
        [
            (rows, channels), (rows, hidden), (rows, hidden), (2, 2 * hidden),
            (2, projection.shape[1]),
        ],
        [ANY] * 11,
        [
            pltpu.VMEM(up.shape, F32),
            pltpu.VMEM(up.shape, F32),
            pltpu.VMEM((2, hidden), F32),
            pltpu.VMEM(down.shape, F32),
            pltpu.VMEM(down.shape, F32),
            pltpu.VMEM((1, channels), F32),
            pltpu.VMEM(projection.shape, F32),
            pltpu.VMEM(image_sum.shape, F32),
            pltpu.SemaphoreType.DMA((6,)),
            pltpu.SemaphoreType.DMA((5,)),
        ],
        us=5.0,
        mib=WIDE,
    )(own, across, up, up_sib, bias, bias_sib, down, down_sib, scale, projection, image_sum)


def normal(rows):
    inverse = lax.rsqrt(jnp.sum(rows * rows, axis=-1, keepdims=True) + 1e-06)
    return rows * inverse, inverse


def pair_kernel(
    mine_ref, other_ref, texts_ref, texts_sib_ref, dp_ref, scale_ref, shift_ref,
    unit_ref, inverse_ref, packed_ref, spread_ref, features, text, text_sib,
):
    embed = unit_ref.shape[1]
    gathered_rows(texts_ref, text)
    gathered_rows(texts_sib_ref, text_sib)
    features[pl.ds(0, 1), :] = mine_ref[pl.ds(0, 1), :] + other_ref[pl.ds(1, 1), :]
    features[pl.ds(1, 1), :] = mine_ref[pl.ds(1, 1), :] + other_ref[pl.ds(0, 1), :]
    unit, inverse = normal(features[...])
    inverse_ref[...] = jnp.broadcast_to(inverse, inverse_ref.shape)
    unit_ref[...] = unit
    spread_rows(unit[0:1], spread_ref, 0)
    spread_rows(unit[1:2], spread_ref, 1)
    step = jnp.zeros(unit.shape, F32)
    losses = jnp.zeros((2, 1), F32)
    for s, block_ref in enumerate((text, text_sib)):
        block, _ = normal(block_ref[...])
        logits = scale_ref[0] * dot(unit, block, ((1,), (1,))) + shift_ref[0]
        if s == 0:
            columns = lax.broadcasted_iota(jnp.int32, logits.shape, 1)
            place = lax.broadcasted_iota(jnp.int32, logits.shape, 0)
            match = jnp.where((place == 0) & (columns == dp_ref[0]), 1.0, 0.0)
        else:
            match = jnp.zeros(logits.shape, F32)
        flipped = (1.0 - 2.0 * match) * logits
        tail = jnp.log1p(jnp.exp(-jnp.abs(flipped)))
        losses = losses + jnp.sum(jnp.maximum(flipped, 0.0) + tail, axis=1, keepdims=True)
        slopes = 1.0 / (1.0 + jnp.exp(-logits)) - match
        step = step + dot(slopes, block)
    packed_ref[:, :embed] = step * scale_ref[0]
    packed_ref[:, embed:] = jnp.broadcast_to(losses, (2, LANES))


def pairs(mine, other, texts, texts_sib, dp, scale, shift):
    embed = mine.shape[1]
    count = texts.size // embed
    return call(
        pair_kernel,
        [(2, embed), (2, LANES), (2, embed + LANES), texts.shape],
        [VMEM] * 4 + [SMEM] * 3,
        [
            pltpu.VMEM(mine.shape, F32),
            pltpu.VMEM((count, embed), F32),
            pltpu.VMEM((count, embed), F32),
        ],
        us=6.0,
    )(mine, other, texts, texts_sib, dp, scale, shift)


def scaled(slope_ref, rows):
    second = lax.broadcasted_iota(jnp.int32, slope_ref.shape, 0) >= slope_ref.shape[0] // 2
    return slope_ref[...] * jnp.where(second, rows[1:2], rows[0:1])


def slope_kernel(
    packed_ref, other_ref, unit_ref, inverse_ref, proj_ref, scale_ref, down_ref, down_sib_ref, up_ref, up_sib_ref,
    slope_ref, slope_sib_ref, loss_ref, const_ref, grad_ref, own_ref, across_ref, sums,
):
    embed = unit_ref.shape[1]
    width = down_ref.shape[0]
    positions = own_ref.shape[0]
    offset = slope_ref.shape[0] // 2
    sums[pl.ds(0, 1), :] = packed_ref[pl.ds(0, 1), :] + other_ref[pl.ds(1, 1), :]
    sums[pl.ds(1, 1), :] = packed_ref[pl.ds(1, 1), :] + other_ref[pl.ds(0, 1), :]
    loss_ref[...] = sums[0:1, embed:]
    step, unit = sums[:, :embed], unit_ref[...]
    grad = step - unit * jnp.sum(unit * step, axis=-1, keepdims=True)
    grad = grad * (inverse_ref[:, 0:1] * (1.0 / positions))
    rows = row_dots(proj_ref, (grad[0:1], grad[1:2]))
    const_ref[...] = rows[0]
    for k in range(2):
        grad_ref[pl.ds(2 + k, 1), :] = rows[k] * scale_ref[...]
    branch = grad_ref[2:4, :]
    for s, weight in enumerate((down_ref, down_sib_ref)):
        for k, row in enumerate(row_dots(weight, (branch[0:1], branch[1:2]))):
            grad_ref[pl.ds(k, 1), s * width : (s + 1) * width] = row
    rows = grad_ref[...]
    total = dot(scaled(slope_ref, rows[:, :width]), up_ref[...], ((1,), (1,)))
    total = total + dot(scaled(slope_sib_ref, rows[:, width:]), up_sib_ref[...], ((1,), (1,)))
    own_ref[...] = total[:positions]
    across_ref[...] = total[offset : offset + positions]


def slopes_of(packed, other, unit, inverse, projection, scale, down, down_sib, up, up_sib, slope, slope_sib, positions):
    channels = up.shape[0]
    return call(
        slope_kernel,
        [(1, LANES), (1, channels), (4, channels), (positions, channels), (positions, channels)],
        [VMEM] * 12,
        [pltpu.VMEM(packed.shape, F32)],
        us=4.0,
        mib=16,
    )(packed, other, unit, inverse, projection, scale[None], down, down_sib, up, up_sib, slope, slope_sib)


def last_kernel(
    both_ref, both_sib_ref, slope_ref, slope_sib_ref, grad_ref, grad_sib_ref, hidden_ref, hidden_sib_ref,
    up_out, down_out,
):
    width = up_out.shape[1]
    rows, rows_sib = grad_ref[...], grad_sib_ref[...]
    up_out[...] = dot(both_ref[...], scaled(slope_ref, rows[:, :width]), ((0,), (0,)))
    up_out[...] += dot(both_sib_ref[...], scaled(slope_sib_ref, rows_sib[:, width:]), ((0,), (0,)))
    down_out[...] = dot(hidden_ref[:, :width], rows[2:4], ((0,), (0,))) + dot(
        hidden_sib_ref[:, width:], rows_sib[2:4], ((0,), (0,))
    )


def last_grads(both, both_sib, slope, slope_sib, grad, grad_sib, hidden, hidden_sib):
    channels, width = both.shape[1], slope.shape[1]
    return call(
        last_kernel, [(channels, width), (width, channels)], [VMEM] * 8, us=0.2, mib=16
    )(both, both_sib, slope, slope_sib, grad, grad_sib, hidden, hidden_sib)


def back_kernel(
    mine_ref, other_any, both_ref, rstd_ref, w_ref, gain_ref, const_ref, out_ref, pad, slope, unit,
    other_ref, sems,
):
    copies = fetch(sems, (other_any, other_ref))
    tiles, side = slope.shape[0], slope.shape[1]
    reach = w_ref.shape[0] // 2
    channels = tiles * LANES
    pad[...] = jnp.zeros_like(pad)
    unit[...] = jnp.zeros_like(unit)
    slope[...] = jnp.zeros_like(slope)
    copies[0].wait()
    first = jnp.zeros((side, 16, LANES), F32)
    second = jnp.zeros((side, 16, LANES), F32)
    for tile in range(tiles):
        lanes = slice(tile * LANES, (tile + 1) * LANES)
        invert = 1.0 / gain_ref[:, lanes]
        for h in range(side):
            rows = slice(h * side, (h + 1) * side)
            unit[tile, h, 0:side, :] = both_ref[rows, lanes] * invert
            slope[tile, h, 0:side, :] = (mine_ref[rows, lanes] + other_ref[rows, lanes]) * gain_ref[:, lanes]
        first = first + slope[tile]
        second = second + slope[tile] * unit[tile]
    first = jnp.sum(first, axis=-1, keepdims=True) * (1.0 / channels)
    second = jnp.sum(second, axis=-1, keepdims=True) * (1.0 / channels)
    rstd = rstd_ref[...]
    for tile in range(tiles):
        grad = rstd * (slope[tile] - first - unit[tile] * second)
        for h in range(side):
            pad[tile, reach + h, pl.ds(reach, side), :] = grad[h, :side]

    @pl.loop(0, tiles)
    def _(tile):
        low, high = convolve(pad, w_ref, tile, side, True)
        slope[tile, :, 0:8, :] = low
        slope[tile, :, 8:16, :] = high

    for tile in range(tiles):
        const = const_ref[:, tile * LANES : (tile + 1) * LANES]
        for h in range(side):
            out_ref[pl.ds(h * side * tiles + tile, side, stride=tiles), :] = (
                slope[tile, h, 0:side, :] + const
            )


def back(mine, other, both, rstd, dw_kernel, norm_gain, const, side):
    taps, channels = dw_kernel.shape[0], dw_kernel.shape[2]
    tiles = channels // LANES
    return call(
        back_kernel,
        [(side * side * tiles, LANES)],
        [VMEM, ANY] + [VMEM] * 5,
        [
            pltpu.VMEM((tiles, side + taps - 1, 24, LANES), F32),
            pltpu.VMEM((tiles, side, 16, LANES), F32),
            pltpu.VMEM((tiles, side, 16, LANES), F32),
            pltpu.VMEM(other.shape, F32),
            pltpu.SemaphoreType.DMA((1,)),
        ],
        us=4.0,
    )(mine, other, both, rstd, dw_kernel, norm_gain, const)[0]


def column_kernel(
    flat_ref, t0_ref, t1_ref, t2_ref, t3_ref, place_ref, scale_ref, shift_ref, o0, o1, o2, o3, images_ref
):
    gathered_rows(flat_ref, images_ref)
    images = images_ref[...]
    for k, (text, out) in enumerate(((t0_ref, o0), (t1_ref, o1), (t2_ref, o2), (t3_ref, o3))):
        unit, _ = normal(text[...])
        logits = scale_ref[0] * jnp.sum(images * unit, axis=-1, keepdims=True) + shift_ref[0]
        slopes = 1.0 / (1.0 + jnp.exp(-logits))
        if k == 0:
            rows = lax.broadcasted_iota(jnp.int32, logits.shape, 0)
            slopes = slopes - jnp.where(rows == place_ref[0], 1.0, 0.0)
        out[...] = jnp.sum(images * (scale_ref[0] * slopes), axis=0, keepdims=True)


def columns_of(images, texts, place, scale, shift):
    embed = texts[0].shape[1]
    return call(
        column_kernel,
        [texts[0].shape] * 4,
        [VMEM] * 5 + [SMEM] * 3,
        [pltpu.VMEM((images.size // embed, embed), F32)],
        us=0.5,
    )(images, *texts, place, scale, shift)


def text_kernel(text_ref, a_ref, b_ref, c_ref, d_ref, out_ref):
    unit, inverse = normal(text_ref[...])
    step = a_ref[...] + b_ref[...] + (c_ref[...] + d_ref[...])
    out_ref[...] = inverse * (step - unit * jnp.sum(unit * step, axis=-1, keepdims=True))


def text_grads(text, parts):
    return call(text_kernel, [text.shape], [VMEM] * 5, us=0.5)(text, *parts)[0]


def swapped(value, by):
    peers = lax.axis_size("fsdp")
    return lax.ppermute(value, "fsdp", [(i, i ^ by) for i in range(peers)])


def mirrored(value):
    peers = lax.axis_size("dp")
    return lax.ppermute(value, "dp", [(i, i ^ 1) for i in range(peers)])


def cornered(value):
    peers, cores = lax.axis_size("dp"), lax.axis_size("fsdp")
    moves = [
        (i * cores + j, (i ^ 1) * cores + (j ^ 1)) for i in range(peers) for j in range(cores)
    ]
    return lax.ppermute(value, ("dp", "fsdp"), moves)


def spread_out(flat):
    peers = lax.axis_size("dp")
    groups = [list(range(start, peers, 2)) for start in range(2)]
    rows = flat.reshape(peers // 2, 1, -1)
    return lax.all_to_all(
        rows, "dp", 0, 0, axis_index_groups=groups, tiled=True
    ).reshape(flat.shape)


def body(
    images,
    dw_kernel,
    norm_gain,
    up_weight,
    up_bias,
    down_weight,
    layer_scale,
    projection,
    text_embed,
    logit_scale,
    logit_bias,
):
    positions = images.shape[1] * images.shape[2]
    peers = lax.axis_size("dp")
    place = (lax.axis_index("dp") // 2 * 2).astype(jnp.int32)[None]
    scale, shift = logit_scale[None], logit_bias[None]
    text_other = mirrored(text_embed)
    normed, rstd, image_sum, gain = front(images, dw_kernel, norm_gain)
    text_other, normed, own_up, own_down, own_bias = lax.optimization_barrier(
        (text_other, normed, up_weight, down_weight, up_bias)
    )
    across = swapped(normed, 2)
    up_sib, down_sib, bias_sib = swapped(own_up, 1), swapped(own_down, 1), swapped(own_bias, 1)
    texts = spread_out(spread_pair(text_embed, text_other, peers))
    positions = images.shape[1] * images.shape[2]
    group_texts = (swapped(text_embed, 1), text_other, swapped(text_other, 1))
    across, group_texts = lax.optimization_barrier((across, group_texts))
    both, slope, slope_sib, hidden, part = mlp(
        normed, across, up_weight, up_sib, up_bias, bias_sib, down_weight, down_sib, layer_scale,
        projection, image_sum, positions,
    )
    part_other = swapped(part, 2)
    texts, hidden = lax.optimization_barrier((texts, hidden))
    texts_sib = swapped(texts, 1)
    image_unit, inverse, packed, image_rows = pairs(
        part, part_other, texts, texts_sib, place, scale, shift
    )
    packed_other = swapped(packed, 2)
    packed, both, slope_sib, hidden = lax.optimization_barrier((packed, both, slope_sib, hidden))
    both_sib, slope_back, hidden_sib = swapped(both, 1), swapped(slope_sib, 1), swapped(hidden, 1)
    losses, const, grad, own_grad, across_grad = slopes_of(
        packed, packed_other, image_unit, inverse, projection, layer_scale,
        down_weight, down_sib, up_weight, up_sib, slope, slope_sib, positions,
    )
    across_grad, image_rows = lax.optimization_barrier((across_grad, image_rows))
    other_grad = swapped(across_grad, 2)
    image_units = spread_out(image_rows)
    up_grad, down_grad = last_grads(
        both, both_sib, slope, slope_back, grad, swapped(grad, 1), hidden, hidden_sib
    )
    other_grad, up_grad = lax.optimization_barrier((other_grad, up_grad))
    input_grad = back(own_grad, other_grad, both, rstd, dw_kernel, gain, const, images.shape[1])
    image_units, input_grad = lax.optimization_barrier((image_units, input_grad))
    steps = columns_of(image_units, (text_embed,) + group_texts, place, scale, shift)
    first_step = steps[0]
    text_grad = text_grads(
        text_embed, (first_step, swapped(steps[1], 1), mirrored(steps[2]), cornered(steps[3]))
    )
    return (
        input_grad.reshape(images.shape),
        up_grad[None],
        down_grad[None],
        text_grad,
        losses[0, :1],
    )


def solution(mesh):
    placed = (
        P(("dp", "fsdp"), None, None, None),
        P(),
        P(),
        P(None, "fsdp"),
        P("fsdp"),
        P("fsdp", None),
        P(),
        P(),
        P(("dp", "fsdp"), None),
        P(),
        P(),
    )
    return jax.shard_map(
        body,
        mesh=mesh,
        in_specs=placed,
        out_specs=(
            P(("dp", "fsdp"), None, None, None),
            P("dp", None, "fsdp"),
            P("dp", "fsdp", None),
            P(("dp", "fsdp"), None),
            P(("dp", "fsdp")),
        ),
        check_vma=False,
    )
```

```python
import functools

import jax
import jax.numpy as jnp
from jax import lax
from jax.experimental import pallas as pl
from jax.experimental.pallas import tpu as pltpu
from jax.sharding import PartitionSpec as P

LANES = 128
HIGH = lax.Precision.HIGH
VMEM = pl.BlockSpec(memory_space=pltpu.VMEM)
SMEM = pl.BlockSpec(memory_space=pltpu.SMEM)
ANY = pl.BlockSpec(memory_space=pl.ANY)
F32 = jnp.float32
WIDE = 55


def call(kernel, outs, specs, scratch=(), us=1.0, mib=12):
    return pl.pallas_call(
        kernel,
        out_shape=[jax.ShapeDtypeStruct(shape, F32) for shape in outs],
        in_specs=specs,
        out_specs=[VMEM] * len(outs),
        scratch_shapes=list(scratch),
        compiler_params=pltpu.CompilerParams(vmem_limit_bytes=mib << 20),
        cost_estimate=pl.CostEstimate(
            flops=int(us * 1.15e9), bytes_accessed=int(us * 3.0e6), transcendentals=0
        ),
    )


def fetch(sems, *pairs):
    copies = [
        pltpu.make_async_copy(source, target, sems.at[i])
        for i, (source, target) in enumerate(pairs)
    ]
    for copy in copies:
        copy.start()
    return copies


def dot(left, right, dims=((1,), (0,))):
    return lax.dot_general(
        left, right, (dims, ((), ())), precision=HIGH, preferred_element_type=F32
    )


def row_dots(matrix_ref, vectors):
    count, width = matrix_ref.shape
    rows = [[] for _ in vectors]
    for block in range(count // LANES):
        for i, vector in enumerate(vectors):
            total = jnp.zeros((LANES, LANES), F32)
            for tile in range(width // LANES):
                lanes = slice(tile * LANES, (tile + 1) * LANES)
                total = total + matrix_ref[block * LANES : (block + 1) * LANES, lanes] * vector[:, lanes]
            rows[i].append(jnp.sum(total.T, axis=0, keepdims=True))
    return [jnp.concatenate(row, axis=1) for row in rows]


def column_dots(vectors, matrix_ref):
    count, width = matrix_ref.shape
    totals = [[None] * (width // LANES) for _ in vectors]
    for block in range(count // LANES):
        rows = slice(block * LANES, (block + 1) * LANES)
        for i, vector in enumerate(vectors):
            column = jnp.broadcast_to(vector[:, rows], (LANES, LANES)).T
            for tile in range(width // LANES):
                term = matrix_ref[rows, tile * LANES : (tile + 1) * LANES] * column
                term = jnp.sum(term.reshape(LANES // 8, 8, LANES), axis=0)
                old = totals[i][tile]
                totals[i][tile] = term if old is None else old + term
    return [
        jnp.concatenate([jnp.sum(part, axis=0, keepdims=True) for part in total], axis=1)
        for total in totals
    ]


def gathered_rows(flat_ref, rows_ref):
    tiles = rows_ref.shape[1] // LANES
    count = rows_ref.shape[0]
    for tile in range(tiles):
        rows_ref[:, tile * LANES : (tile + 1) * LANES] = flat_ref[pl.ds(tile, count, stride=tiles), :]


def lanes_of(tile):
    return pl.ds(pl.multiple_of(tile * LANES, LANES), LANES)


def convolve(pad, w_ref, tile, side, flip):
    taps = w_ref.shape[0]
    halves = []
    for half in range(2):
        total = jnp.zeros((side, 8, LANES), F32)
        for q in range(taps):
            column = pad[tile, :, pl.ds(q + 8 * half, 8), :]
            for p in range(taps):
                row = taps - 1 - p if flip else p
                col = taps - 1 - q if flip else q
                total = total + column[p : p + side] * w_ref[row, pl.ds(col, 1), lanes_of(tile)]
        halves.append(total)
    return halves


def front_kernel(
    x_any, w_any, gain_any, normed_ref, rstd_ref, sum_ref, gain_ref, x_ref, w_ref, pad, mixed, sems
):
    tiles, side = mixed.shape[0], mixed.shape[1]
    reach = w_ref.shape[0] // 2
    channels = tiles * LANES
    copies = fetch(sems, (x_any, x_ref), (w_any, w_ref), (gain_any, gain_ref.at[0]))
    pad[...] = jnp.zeros_like(pad)
    for copy in copies:
        copy.wait()
    for tile in range(tiles):
        total = jnp.zeros((side, LANES), F32)
        for h in range(side):
            row = x_ref[pl.ds(h * side * tiles + tile, side, stride=tiles), :]
            pad[tile, reach + h, pl.ds(reach, side), :] = row
            total = total + row
        sum_ref[:, tile * LANES : (tile + 1) * LANES] = jnp.sum(total, axis=0, keepdims=True)

    @pl.loop(0, tiles)
    def _(tile):
        low, high = convolve(pad, w_ref, tile, side, False)
        mixed[tile, :, 0:8, :] = low
        mixed[tile, :, 8:16, :] = high

    total = mixed[0]
    for tile in range(1, tiles):
        total = total + mixed[tile]
    mean = jnp.sum(total, axis=-1, keepdims=True) * (1.0 / channels)
    square = jnp.zeros((side, 16, LANES), F32)
    for tile in range(tiles):
        off = mixed[tile] - mean
        square = square + off * off
    rstd = lax.rsqrt(jnp.sum(square, axis=-1, keepdims=True) * (1.0 / channels) + 1e-06)
    rstd_ref[...] = jnp.broadcast_to(rstd, rstd_ref.shape)
    for tile in range(tiles):
        lanes = slice(tile * LANES, (tile + 1) * LANES)
        out = (mixed[tile] - mean) * rstd * gain_ref[:, lanes]
        for h in range(side):
            normed_ref[h * side : (h + 1) * side, lanes] = out[h, :side]
    rest = normed_ref.shape[0] - side * side
    normed_ref[side * side :, :] = jnp.zeros((rest, channels), F32)


def front(images, dw_kernel, norm_gain):
    side, taps = images.shape[1], dw_kernel.shape[0]
    channels = images.shape[3]
    tiles = channels // LANES
    return call(
        front_kernel,
        [
            (pl.cdiv(side * side, 8) * 8, channels),
            (side, 16, LANES),
            (1, channels),
            (1, channels),
        ],
        [ANY] * 3,
        [
            pltpu.VMEM((side * side * tiles, LANES), F32),
            pltpu.VMEM(dw_kernel.shape, F32),
            pltpu.VMEM((tiles, side + taps - 1, 24, LANES), F32),
            pltpu.VMEM((tiles, side, 16, LANES), F32),
            pltpu.SemaphoreType.DMA((3,)),
        ],
        us=4.0,
        mib=WIDE,
    )(images.reshape(-1, LANES), dw_kernel, norm_gain)


def spread_rows(row, out_ref, place):
    tiles = row.shape[1] // LANES
    copies = out_ref.shape[0] // (2 * tiles)
    for tile in range(tiles):
        out_ref[pl.ds(place * tiles + tile, copies, stride=2 * tiles), :] = jnp.broadcast_to(
            row[:, tile * LANES : (tile + 1) * LANES], (copies, LANES)
        )


def spread_kernel(row_ref, other_ref, out_ref):
    spread_rows(row_ref[...], out_ref, 0)
    spread_rows(other_ref[...], out_ref, 1)


def spread_pair(row, other, peers):
    flat = (peers * row.shape[1] // LANES, LANES)
    return call(spread_kernel, [flat], [VMEM] * 2, us=0.5)(row, other)[0]


def mlp_kernel(
    own_any, across_any, up_any, up_sib_any, bias_any, bias_sib_any, down_any, down_sib_any, scale_any, proj_any,
    sum_any, both_ref, slope_ref, slope_sib_ref, hidden_ref, part_ref,
    up_ref, up_sib_ref, bias_ref, down_ref, down_sib_ref, scale_ref, proj_ref, sum_ref, sems, late_sems,
    *, positions,
):
    offset = own_any.shape[0]
    width = up_ref.shape[1]
    copies = fetch(
        sems,
        (own_any, both_ref.at[pl.ds(0, offset)]),
        (across_any, both_ref.at[pl.ds(offset, offset)]),
        (up_any, up_ref),
        (bias_any, bias_ref.at[0]),
        (bias_sib_any, bias_ref.at[1]),
        (up_sib_any, up_sib_ref),
    )
    for copy in copies[:5]:
        copy.wait()
    late = fetch(
        late_sems,
        (scale_any, scale_ref.at[0]),
        (sum_any, sum_ref),
        (down_any, down_ref),
        (down_sib_any, down_sib_ref),
        (proj_any, proj_ref),
    )
    for s, (weight, out) in enumerate(((up_ref, slope_ref), (up_sib_ref, slope_sib_ref))):
        if s == 1:
            copies[5].wait()
        pre = dot(both_ref[...], weight[...]) + bias_ref[pl.ds(s, 1), :]
        cdf = 0.5 * (1.0 + lax.erf(pre * (0.5**0.5)))
        out[...] = cdf + pre * (jnp.exp(-0.5 * pre * pre) * 0.3989422804014327)
        act = pre * cdf
        for k in range(2):
            hidden_ref[pl.ds(k, 1), s * width : (s + 1) * width] = jnp.sum(
                act[k * offset : k * offset + positions], axis=0, keepdims=True
            )
    hidden = hidden_ref[...]
    for copy in late[:4]:
        copy.wait()
    first = column_dots((hidden[0:1, :width], hidden[1:2, :width]), down_ref)
    second = column_dots((hidden[0:1, width:], hidden[1:2, width:]), down_sib_ref)
    pooled = []
    for k in range(2):
        row = (first[k] + second[k]) * scale_ref[...]
        pooled.append((row + sum_ref[...] if k == 0 else row) * (1.0 / positions))
    late[4].wait()
    for k, row in enumerate(column_dots(pooled, proj_ref)):
        part_ref[pl.ds(k, 1), :] = row


def mlp(own, across, up, up_sib, bias, bias_sib, down, down_sib, scale, projection, image_sum, positions):
    channels = own.shape[1]
    hidden = up.shape[1]
    rows = 2 * own.shape[0]
    return call(
        functools.partial(mlp_kernel, positions=positions),
        [
            (rows, channels), (rows, hidden), (rows, hidden), (2, 2 * hidden),
            (2, projection.shape[1]),
        ],
        [ANY] * 11,
        [
            pltpu.VMEM(up.shape, F32),
            pltpu.VMEM(up.shape, F32),
            pltpu.VMEM((2, hidden), F32),
            pltpu.VMEM(down.shape, F32),
            pltpu.VMEM(down.shape, F32),
            pltpu.VMEM((1, channels), F32),
            pltpu.VMEM(projection.shape, F32),
            pltpu.VMEM(image_sum.shape, F32),
            pltpu.SemaphoreType.DMA((6,)),
            pltpu.SemaphoreType.DMA((5,)),
        ],
        us=5.0,
        mib=WIDE,
    )(own, across, up, up_sib, bias, bias_sib, down, down_sib, scale, projection, image_sum)


def normal(rows):
    inverse = lax.rsqrt(jnp.sum(rows * rows, axis=-1, keepdims=True) + 1e-06)
    return rows * inverse, inverse


def pair_kernel(
    mine_ref, other_ref, texts_ref, texts_sib_ref, dp_ref, scale_ref, shift_ref,
    unit_ref, inverse_ref, packed_ref, spread_ref, features, text, text_sib,
):
    embed = unit_ref.shape[1]
    gathered_rows(texts_ref, text)
    gathered_rows(texts_sib_ref, text_sib)
    features[pl.ds(0, 1), :] = mine_ref[pl.ds(0, 1), :] + other_ref[pl.ds(1, 1), :]
    features[pl.ds(1, 1), :] = mine_ref[pl.ds(1, 1), :] + other_ref[pl.ds(0, 1), :]
    unit, inverse = normal(features[...])
    inverse_ref[...] = jnp.broadcast_to(inverse, inverse_ref.shape)
    unit_ref[...] = unit
    spread_rows(unit[0:1], spread_ref, 0)
    spread_rows(unit[1:2], spread_ref, 1)
    step = jnp.zeros(unit.shape, F32)
    losses = jnp.zeros((2, 1), F32)
    for s, block_ref in enumerate((text, text_sib)):
        block, _ = normal(block_ref[...])
        logits = scale_ref[0] * dot(unit, block, ((1,), (1,))) + shift_ref[0]
        if s == 0:
            columns = lax.broadcasted_iota(jnp.int32, logits.shape, 1)
            place = lax.broadcasted_iota(jnp.int32, logits.shape, 0)
            match = jnp.where((place == 0) & (columns == dp_ref[0]), 1.0, 0.0)
        else:
            match = jnp.zeros(logits.shape, F32)
        flipped = (1.0 - 2.0 * match) * logits
        tail = jnp.log1p(jnp.exp(-jnp.abs(flipped)))
        losses = losses + jnp.sum(jnp.maximum(flipped, 0.0) + tail, axis=1, keepdims=True)
        slopes = 1.0 / (1.0 + jnp.exp(-logits)) - match
        step = step + dot(slopes, block)
    packed_ref[:, :embed] = step * scale_ref[0]
    packed_ref[:, embed:] = jnp.broadcast_to(losses, (2, LANES))


def pairs(mine, other, texts, texts_sib, dp, scale, shift):
    embed = mine.shape[1]
    count = texts.size // embed
    return call(
        pair_kernel,
        [(2, embed), (2, LANES), (2, embed + LANES), texts.shape],
        [VMEM] * 4 + [SMEM] * 3,
        [
            pltpu.VMEM(mine.shape, F32),
            pltpu.VMEM((count, embed), F32),
            pltpu.VMEM((count, embed), F32),
        ],
        us=14.0,
    )(mine, other, texts, texts_sib, dp, scale, shift)


def scaled(slope_ref, rows):
    second = lax.broadcasted_iota(jnp.int32, slope_ref.shape, 0) >= slope_ref.shape[0] // 2
    return slope_ref[...] * jnp.where(second, rows[1:2], rows[0:1])


def slope_kernel(
    packed_ref, other_ref, unit_ref, inverse_ref, proj_ref, scale_ref, down_ref, down_sib_ref, up_ref, up_sib_ref,
    slope_ref, slope_sib_ref, hidden_ref, loss_ref, const_ref, grad_ref, own_ref, across_ref, sums,
):
    embed = unit_ref.shape[1]
    width = down_ref.shape[0]
    positions = own_ref.shape[0]
    offset = slope_ref.shape[0] // 2
    sums[pl.ds(0, 1), :] = packed_ref[pl.ds(0, 1), :] + other_ref[pl.ds(1, 1), :]
    sums[pl.ds(1, 1), :] = packed_ref[pl.ds(1, 1), :] + other_ref[pl.ds(0, 1), :]
    loss_ref[...] = sums[0:1, embed:]
    step, unit = sums[:, :embed], unit_ref[...]
    grad = step - unit * jnp.sum(unit * step, axis=-1, keepdims=True)
    grad = grad * (inverse_ref[:, 0:1] * (1.0 / positions))
    rows = row_dots(proj_ref, (grad[0:1], grad[1:2]))
    const_ref[...] = rows[0]
    for k in range(2):
        grad_ref[pl.ds(2 + k, 1), :] = rows[k] * scale_ref[...]
    branch = grad_ref[2:4, :]
    grad_ref[4:6, :] = hidden_ref[...]
    for s, weight in enumerate((down_ref, down_sib_ref)):
        for k, row in enumerate(row_dots(weight, (branch[0:1], branch[1:2]))):
            grad_ref[pl.ds(k, 1), s * width : (s + 1) * width] = row
    rows = grad_ref[...]
    total = dot(scaled(slope_ref, rows[:, :width]), up_ref[...], ((1,), (1,)))
    total = total + dot(scaled(slope_sib_ref, rows[:, width:]), up_sib_ref[...], ((1,), (1,)))
    own_ref[...] = total[:positions]
    across_ref[...] = total[offset : offset + positions]


def slopes_of(packed, other, unit, inverse, projection, scale, down, down_sib, up, up_sib, slope, slope_sib, hidden, positions):
    channels = up.shape[0]
    return call(
        slope_kernel,
        [(1, LANES), (1, channels), (6, channels), (positions, channels), (positions, channels)],
        [VMEM] * 13,
        [pltpu.VMEM(packed.shape, F32)],
        us=4.0,
        mib=16,
    )(packed, other, unit, inverse, projection, scale[None], down, down_sib, up, up_sib, slope, slope_sib, hidden)


def last_kernel(
    both_ref, both_sib_ref, slope_ref, slope_sib_ref, grad_ref, grad_sib_ref,
    up_out, down_out,
):
    width = up_out.shape[1]
    rows, rows_sib = grad_ref[...], grad_sib_ref[...]
    up_out[...] = dot(both_ref[...], scaled(slope_ref, rows[:, :width]), ((0,), (0,)))
    up_out[...] += dot(both_sib_ref[...], scaled(slope_sib_ref, rows_sib[:, width:]), ((0,), (0,)))
    down_out[...] = dot(rows[4:6, :width], rows[2:4], ((0,), (0,))) + dot(
        rows_sib[4:6, width:], rows_sib[2:4], ((0,), (0,))
    )


def last_grads(both, both_sib, slope, slope_sib, grad, grad_sib):
    channels, width = both.shape[1], slope.shape[1]
    return call(
        last_kernel, [(channels, width), (width, channels)], [VMEM] * 6, us=0.2, mib=16
    )(both, both_sib, slope, slope_sib, grad, grad_sib)


def back_kernel(
    mine_ref, other_any, both_ref, rstd_ref, w_ref, gain_ref, const_ref, out_ref, pad, slope, unit,
    other_ref, sems,
):
    copies = fetch(sems, (other_any, other_ref))
    tiles, side = slope.shape[0], slope.shape[1]
    reach = w_ref.shape[0] // 2
    channels = tiles * LANES
    pad[...] = jnp.zeros_like(pad)
    unit[...] = jnp.zeros_like(unit)
    slope[...] = jnp.zeros_like(slope)
    copies[0].wait()
    first = jnp.zeros((side, 16, LANES), F32)
    second = jnp.zeros((side, 16, LANES), F32)
    for tile in range(tiles):
        lanes = slice(tile * LANES, (tile + 1) * LANES)
        invert = 1.0 / gain_ref[:, lanes]
        for h in range(side):
            rows = slice(h * side, (h + 1) * side)
            unit[tile, h, 0:side, :] = both_ref[rows, lanes] * invert
            slope[tile, h, 0:side, :] = (mine_ref[rows, lanes] + other_ref[rows, lanes]) * gain_ref[:, lanes]
        first = first + slope[tile]
        second = second + slope[tile] * unit[tile]
    first = jnp.sum(first, axis=-1, keepdims=True) * (1.0 / channels)
    second = jnp.sum(second, axis=-1, keepdims=True) * (1.0 / channels)
    rstd = rstd_ref[...]
    for tile in range(tiles):
        grad = rstd * (slope[tile] - first - unit[tile] * second)
        for h in range(side):
            pad[tile, reach + h, pl.ds(reach, side), :] = grad[h, :side]

    @pl.loop(0, tiles)
    def _(tile):
        low, high = convolve(pad, w_ref, tile, side, True)
        slope[tile, :, 0:8, :] = low
        slope[tile, :, 8:16, :] = high

    for tile in range(tiles):
        const = const_ref[:, tile * LANES : (tile + 1) * LANES]
        for h in range(side):
            out_ref[pl.ds(h * side * tiles + tile, side, stride=tiles), :] = (
                slope[tile, h, 0:side, :] + const
            )


def back(mine, other, both, rstd, dw_kernel, norm_gain, const, side):
    taps, channels = dw_kernel.shape[0], dw_kernel.shape[2]
    tiles = channels // LANES
    return call(
        back_kernel,
        [(side * side * tiles, LANES)],
        [VMEM, ANY] + [VMEM] * 5,
        [
            pltpu.VMEM((tiles, side + taps - 1, 24, LANES), F32),
            pltpu.VMEM((tiles, side, 16, LANES), F32),
            pltpu.VMEM((tiles, side, 16, LANES), F32),
            pltpu.VMEM(other.shape, F32),
            pltpu.SemaphoreType.DMA((1,)),
        ],
        us=4.0,
    )(mine, other, both, rstd, dw_kernel, norm_gain, const)[0]


def column_kernel(
    flat_ref, t0_ref, t1_ref, t2_ref, t3_ref, place_ref, scale_ref, shift_ref, o0, o1, o2, o3, images_ref
):
    gathered_rows(flat_ref, images_ref)
    images = images_ref[...]
    for k, (text, out) in enumerate(((t0_ref, o0), (t1_ref, o1), (t2_ref, o2), (t3_ref, o3))):
        unit, _ = normal(text[...])
        logits = scale_ref[0] * jnp.sum(images * unit, axis=-1, keepdims=True) + shift_ref[0]
        slopes = 1.0 / (1.0 + jnp.exp(-logits))
        if k == 0:
            rows = lax.broadcasted_iota(jnp.int32, logits.shape, 0)
            slopes = slopes - jnp.where(rows == place_ref[0], 1.0, 0.0)
        out[...] = jnp.sum(images * (scale_ref[0] * slopes), axis=0, keepdims=True)


def columns_of(images, texts, place, scale, shift):
    embed = texts[0].shape[1]
    return call(
        column_kernel,
        [texts[0].shape] * 4,
        [VMEM] * 5 + [SMEM] * 3,
        [pltpu.VMEM((images.size // embed, embed), F32)],
        us=0.5,
    )(images, *texts, place, scale, shift)


def text_kernel(text_ref, a_ref, b_ref, c_ref, d_ref, out_ref):
    unit, inverse = normal(text_ref[...])
    step = a_ref[...] + b_ref[...] + (c_ref[...] + d_ref[...])
    out_ref[...] = inverse * (step - unit * jnp.sum(unit * step, axis=-1, keepdims=True))


def text_grads(text, parts):
    return call(text_kernel, [text.shape], [VMEM] * 5, us=0.5)(text, *parts)[0]


def swapped(value, by):
    peers = lax.axis_size("fsdp")
    return lax.ppermute(value, "fsdp", [(i, i ^ by) for i in range(peers)])


def mirrored(value):
    peers = lax.axis_size("dp")
    return lax.ppermute(value, "dp", [(i, i ^ 1) for i in range(peers)])


def cornered(value):
    peers, cores = lax.axis_size("dp"), lax.axis_size("fsdp")
    moves = [
        (i * cores + j, (i ^ 1) * cores + (j ^ 1)) for i in range(peers) for j in range(cores)
    ]
    return lax.ppermute(value, ("dp", "fsdp"), moves)


def spread_out(flat):
    peers = lax.axis_size("dp")
    groups = [list(range(start, peers, 2)) for start in range(2)]
    rows = flat.reshape(peers // 2, 1, -1)
    return lax.all_to_all(
        rows, "dp", 0, 0, axis_index_groups=groups, tiled=True
    ).reshape(flat.shape)


def body(
    images,
    dw_kernel,
    norm_gain,
    up_weight,
    up_bias,
    down_weight,
    layer_scale,
    projection,
    text_embed,
    logit_scale,
    logit_bias,
):
    positions = images.shape[1] * images.shape[2]
    peers = lax.axis_size("dp")
    place = (lax.axis_index("dp") // 2 * 2).astype(jnp.int32)[None]
    scale, shift = logit_scale[None], logit_bias[None]
    text_other = mirrored(text_embed)
    normed, rstd, image_sum, gain = front(images, dw_kernel, norm_gain)
    text_other, normed, own_up, own_down, own_bias = lax.optimization_barrier(
        (text_other, normed, up_weight, down_weight, up_bias)
    )
    across = swapped(normed, 2)
    up_sib, down_sib, bias_sib = swapped(own_up, 1), swapped(own_down, 1), swapped(own_bias, 1)
    texts = spread_out(spread_pair(text_embed, text_other, peers))
    positions = images.shape[1] * images.shape[2]
    group_texts = (swapped(text_embed, 1), text_other, swapped(text_other, 1))
    across, group_texts = lax.optimization_barrier((across, group_texts))
    both, slope, slope_sib, hidden, part = mlp(
        normed, across, up_weight, up_sib, up_bias, bias_sib, down_weight, down_sib, layer_scale,
        projection, image_sum, positions,
    )
    part_other = swapped(part, 2)
    texts, hidden = lax.optimization_barrier((texts, hidden))
    texts_sib = swapped(texts, 1)
    image_unit, inverse, packed, image_rows = pairs(
        part, part_other, texts, texts_sib, place, scale, shift
    )
    packed_other = swapped(packed, 2)
    both_sib = swapped(both, 1)
    packed, slope_sib = lax.optimization_barrier((packed, slope_sib))
    slope_back = swapped(slope_sib, 1)
    losses, const, grad, own_grad, across_grad = slopes_of(
        packed, packed_other, image_unit, inverse, projection, layer_scale,
        down_weight, down_sib, up_weight, up_sib, slope, slope_sib, hidden, positions,
    )
    across_grad, image_rows = lax.optimization_barrier((across_grad, image_rows))
    other_grad = swapped(across_grad, 2)
    image_units = spread_out(image_rows)
    up_grad, down_grad = last_grads(
        both, both_sib, slope, slope_back, grad, swapped(grad, 1)
    )
    other_grad, up_grad = lax.optimization_barrier((other_grad, up_grad))
    input_grad = back(own_grad, other_grad, both, rstd, dw_kernel, gain, const, images.shape[1])
    image_units, input_grad = lax.optimization_barrier((image_units, input_grad))
    steps = columns_of(image_units, (text_embed,) + group_texts, place, scale, shift)
    first_step = steps[0]
    text_grad = text_grads(
        text_embed, (first_step, swapped(steps[1], 1), mirrored(steps[2]), cornered(steps[3]))
    )
    return (
        input_grad.reshape(images.shape),
        up_grad[None],
        down_grad[None],
        text_grad,
        losses[0, :1],
    )


def solution(mesh):
    placed = (
        P(("dp", "fsdp"), None, None, None),
        P(),
        P(),
        P(None, "fsdp"),
        P("fsdp"),
        P("fsdp", None),
        P(),
        P(),
        P(("dp", "fsdp"), None),
        P(),
        P(),
    )
    return jax.shard_map(
        body,
        mesh=mesh,
        in_specs=placed,
        out_specs=(
            P(("dp", "fsdp"), None, None, None),
            P("dp", None, "fsdp"),
            P("dp", "fsdp", None),
            P(("dp", "fsdp"), None),
            P(("dp", "fsdp")),
        ),
        check_vma=False,
    )
```
